32 devices in a mesh: dp: 4 (over z), ctx: 8 (over y, x, core).
Axes of the slice: x: 2, y: 2, z: 4, core: 2. Of those that a mesh axis runs over, the one named last changes fastest.
Arguments:
- values: bfloat16 [4, 1024, 512], P('dp', 'ctx'), may hold values from -6 to 6
- gates: bfloat16 [4, 1024, 512], P('dp', 'ctx'), may hold values from -6 to 6
- grad_out: bfloat16 [4, 1024, 512], P('dp', 'ctx'), may hold values from -6 to 6
- filters: float32 [512, 1024], P('ctx'), may hold values from -6 to 6
- skip: float32 [512], P('ctx'), may hold values from 0.5 to 1.5
Outputs:
- grad_values: bfloat16 [4, 1024, 512], P('dp', 'ctx')
- grad_gates: bfloat16 [4, 1024, 512], P('dp', 'ctx')
- grad_filters: float32 [512, 1024], P('ctx')
The draws below stay inside these ranges and needn't reach their ends.
All inputs are finite; a program needn't handle non-finite values.
Results may differ from the reference program's by a relative error of at most 0.0049.
Values may be sent and summed in bfloat16 or wider, within the bound.
No kernel may reach another device: no remote copies, remote signals or barrier semaphores. Data moves between devices by JAX's collectives and lax.ppermute only.
A program may use at most 64 MiB of HBM per device.

```python
import jax
import jax.numpy as jnp
from jax import lax

CH = 512
LENGTH = 1024
SEQS = 4


def block_levels(stream_key, extent, cuts, least, largest):
    level = 1.0
    for axis_at, shards_of in cuts:
        heights = jax.random.uniform(jax.random.fold_in(jax.random.fold_in(stream_key, 6), axis_at), (shards_of,), jnp.float32, least / len(cuts), largest / len(cuts))
        level = level * jnp.repeat(jnp.exp(heights), extent[axis_at] // shards_of).reshape((-1,) + (1,) * (len(extent) - 1 - axis_at))
    return level


def bell_draw(own_key, extent, spread, most, pieces=(), dtype=jnp.bfloat16):
    factor_of = block_levels(own_key, extent, pieces, -0.22, 0.18) if pieces else 1.0
    drawn = jax.random.normal(own_key, extent, jnp.float32) * spread * factor_of
    return jnp.minimum(jnp.maximum(drawn, -most), most).astype(dtype)


def setup_inputs(seed: int = 0) -> dict:
    splits = jax.random.split(jax.random.key(seed), 6)
    values = bell_draw(splits[0], (SEQS, LENGTH, CH), 1.0, 6.0, ((0, 4), (1, 8)))
    gates = bell_draw(splits[1], (SEQS, LENGTH, CH), 1.0, 6.0, ((0, 4), (1, 8)))
    grad_out = bell_draw(splits[2], (SEQS, LENGTH, CH), 1.0, 6.0, ((0, 4), (1, 8)))
    filters = bell_draw(splits[3], (CH, LENGTH), 1.0, 6.0, ((0, 8),), jnp.float32)
    skip = jnp.clip(0.5 + 1.0 * jax.random.uniform(splits[4], (CH,), jnp.float32) ** block_levels(splits[4], (CH,), ((0, 8),), -0.2, 0.2), 0.5, 1.5)
    return {"values": values, "gates": gates, "grad_out": grad_out, "filters": filters, "skip": skip}


def reference(values, gates, grad_out, filters, skip):
    length = values.shape[1]
    count = 2 * length
    scale_a = length ** -0.5
    scale_b = (values.shape[0] * length) ** -0.5
    filt_spec = jnp.fft.rfft(filters, n=count, axis=1)
    gains = skip[:, None]

    def one_seq(total, inputs):
        vals, gate, grad = inputs
        grad_f = grad.astype(jnp.float32)
        grad_conv = (grad_f * gate.astype(jnp.float32)).astype(jnp.bfloat16)
        grad_conv = lax.optimization_barrier(grad_conv)
        vals_t = vals.astype(jnp.float32).T
        dz_t = grad_conv.astype(jnp.float32).T
        vals_spec = jnp.fft.rfft(vals_t, n=count, axis=1)
        dz_spec = jnp.fft.rfft(dz_t, n=count, axis=1)
        conv_raw = jnp.fft.irfft(filt_spec * vals_spec, n=count, axis=1)[:, :length]
        conv = (scale_a * conv_raw + gains * vals_t).astype(jnp.bfloat16)
        conv = lax.optimization_barrier(conv)
        grad_gate = (grad_f * conv.astype(jnp.float32).T).astype(jnp.bfloat16)
        corr = jnp.fft.irfft(jnp.conj(filt_spec) * dz_spec, n=count, axis=1)[:, :length]
        grad_val = (scale_a * corr + gains * dz_t).T.astype(jnp.bfloat16)
        cross = jnp.fft.irfft(jnp.conj(vals_spec) * dz_spec, n=count, axis=1)[:, :length]
        return total + cross, (grad_val, grad_gate)

    start = jnp.zeros(filters.shape, jnp.float32)
    total, (grad_values, grad_gates) = lax.scan(one_seq, start, (values, gates, grad_out))
    return grad_values, grad_gates, scale_b * total
```

```python
import functools
import math

import jax
import jax.numpy as jnp
import numpy as np
from jax import lax
from jax.experimental import pallas as pl
from jax.experimental.pallas import tpu as pltpu
from jax.sharding import PartitionSpec as P

HIGH = lax.Precision.HIGHEST
BF16 = jnp.bfloat16
F32 = jnp.float32
DENSE_LIMIT = 1024
VMEM_BYTES = 48 * 2**20


def twiddle(rows, cols, period):
    left = lax.broadcasted_iota(jnp.int32, (rows, cols), 0)
    right = lax.broadcasted_iota(jnp.int32, (rows, cols), 1)
    angle = (left * right % period).astype(jnp.float32) * (2.0 * math.pi / period)
    return (jnp.cos(angle), jnp.sin(angle))


def pick_first(period):
    best = 2
    for cand in range(2, math.isqrt(period) + 1):
        if period % cand == 0 and cand % 2 == 0:
            best = cand
    return best


def make_tables(length):
    period = 2 * length
    first = pick_first(period)
    second = period // first
    half = first // 2
    return (
        twiddle(half, first, first),
        twiddle(first, second, period),
        twiddle(second, second, second),
        half,
        first,
        second,
        period,
    )


def forward(signal, tables):
    (cos_one, sin_one), (cos_mid, sin_mid), (cos_two, sin_two), half, first, second, period = tables
    shaped = signal.reshape(signal.shape[0], half, second)
    part_re = jnp.einsum("cmn,mk->ckn", shaped, cos_one, precision=HIGH)
    part_im = -jnp.einsum("cmn,mk->ckn", shaped, sin_one, precision=HIGH)
    mid_re = part_re * cos_mid + part_im * sin_mid
    mid_im = part_im * cos_mid - part_re * sin_mid
    spec_re = jnp.einsum("ckn,nm->ckm", mid_re, cos_two, precision=HIGH) + jnp.einsum(
        "ckn,nm->ckm", mid_im, sin_two, precision=HIGH
    )
    spec_im = jnp.einsum("ckn,nm->ckm", mid_im, cos_two, precision=HIGH) - jnp.einsum(
        "ckn,nm->ckm", mid_re, sin_two, precision=HIGH
    )
    return (spec_re, spec_im)


def inverse(spec_re, spec_im, tables):
    (cos_one, sin_one), (cos_mid, sin_mid), (cos_two, sin_two), half, first, second, period = tables
    back_re = jnp.einsum("ckm,nm->ckn", spec_re, cos_two, precision=HIGH) - jnp.einsum(
        "ckm,nm->ckn", spec_im, sin_two, precision=HIGH
    )
    back_im = jnp.einsum("ckm,nm->ckn", spec_im, cos_two, precision=HIGH) + jnp.einsum(
        "ckm,nm->ckn", spec_re, sin_two, precision=HIGH
    )
    turned_re = back_re * cos_mid - back_im * sin_mid
    turned_im = back_im * cos_mid + back_re * sin_mid
    result = jnp.einsum("ckn,mk->cmn", turned_re, cos_one, precision=HIGH) - jnp.einsum(
        "ckn,mk->cmn", turned_im, sin_one, precision=HIGH
    )
    return result.reshape(spec_re.shape[0], half * second) * (1.0 / period)


def spectral(vals_f, dz_f, filt, gains, tables, scale_a):
    vals_re, vals_im = forward(vals_f, tables)
    dz_re, dz_im = forward(dz_f, tables)
    filt_re, filt_im = forward(filt, tables)
    conv_raw = inverse(
        filt_re * vals_re - filt_im * vals_im, filt_re * vals_im + filt_im * vals_re, tables
    )
    conv = (scale_a * conv_raw + gains * vals_f).astype(BF16)
    corr = inverse(filt_re * dz_re + filt_im * dz_im, filt_re * dz_im - filt_im * dz_re, tables)
    grad_val = (scale_a * corr + gains * dz_f).astype(BF16)
    cross = inverse(vals_re * dz_re + vals_im * dz_im, vals_re * dz_im - vals_im * dz_re, tables)
    return (grad_val, conv, cross)


def per_device_long(values, gates, grad_out, filters, skip):
    length = filters.shape[1]
    scale_a = length ** (-0.5)
    scale_b = (lax.axis_size("dp") * length) ** (-0.5)
    tok_grad = grad_out[0].astype(F32)
    dz_tok = (tok_grad * gates[0].astype(F32)).astype(BF16)
    vals_ch, dz_ch = (
        lax.all_to_all(values[0].T, "ctx", split_axis=0, concat_axis=1, tiled=True),
        lax.all_to_all(dz_tok.T, "ctx", split_axis=0, concat_axis=1, tiled=True),
    )
    grad_val, conv, cross = spectral(
        vals_ch.astype(F32),
        dz_ch.astype(F32),
        filters,
        skip[:, None],
        make_tables(length),
        scale_a,
    )
    total = lax.psum(cross, "dp")
    val_back, conv_back = (
        lax.all_to_all(grad_val, "ctx", split_axis=1, concat_axis=0, tiled=True),
        lax.all_to_all(conv, "ctx", split_axis=1, concat_axis=0, tiled=True),
    )
    grad_gate_tok = (tok_grad * conv_back.T.astype(F32)).astype(BF16)
    return (val_back.T[None], grad_gate_tok[None], scale_b * total)


def dense_tables(length):
    n = np.arange(length, dtype=np.int64)[:, None]
    k = np.arange(length, dtype=np.int64)[None, :]
    angle = ((2 * k + 1) * n % (4 * length)).astype(np.float64) * (math.pi / (2 * length))
    full = np.concatenate([np.cos(angle), -np.sin(angle)], axis=1)
    high = full.astype(BF16)
    low = (full - high.astype(np.float64)).astype(BF16)
    return high, low, np.ascontiguousarray(high.T)


def vmem_specs(count):
    return [pl.BlockSpec(memory_space=pltpu.VMEM)] * count


def in_vmem(array):
    return pltpu.with_memory_space_constraint(array, pltpu.VMEM)


def pack_kernel(parts, vals_ref, gate_ref, grad_ref, out_ref):
    chans = vals_ref.shape[2] // parts
    vals = vals_ref[0].astype(F32).T.astype(BF16)
    dz = (grad_ref[0].astype(F32) * gate_ref[0].astype(F32)).T.astype(BF16)
    for d in range(parts):
        out_ref[d, :chans, :] = vals[d * chans : (d + 1) * chans, :]
        out_ref[d, chans:, :] = dz[d * chans : (d + 1) * chans, :]


def filter_kernel(filt_ref, high_ref, low_ref, out_ref):
    filt = filt_ref[...]
    f_high = filt.astype(BF16)
    f_low = (filt - f_high.astype(F32)).astype(BF16)
    high = high_ref[...]
    total = jnp.dot(f_high, low_ref[...], preferred_element_type=F32)
    total = total + jnp.dot(f_low, high, preferred_element_type=F32)
    out_ref[...] = total + jnp.dot(f_high, high, preferred_element_type=F32)


def main_kernel(x_ref, fwd_ref, inv_ref, filt_ref, skip_ref, back_ref, cross_ref):
    parts, rows, pos = x_ref.shape
    chans = rows // 2
    length = parts * pos
    x = jnp.concatenate([x_ref[s] for s in range(parts)], axis=1)
    spec = jnp.dot(x, fwd_ref[...], preferred_element_type=F32)
    vr, vi = spec[:chans, :length], spec[:chans, length:]
    gr, gi = spec[chans:, :length], spec[chans:, length:]
    hr, hi = filt_ref[:, :length], filt_ref[:, length:]
    real = jnp.concatenate([hr * vr - hi * vi, hr * gr + hi * gi, vr * gr + vi * gi], axis=0)
    imag = jnp.concatenate([hr * vi + hi * vr, hr * gi - hi * gr, vr * gi - vi * gr], axis=0)
    prod = jnp.concatenate([real.astype(BF16), imag.astype(BF16)], axis=1)
    res = jnp.dot(prod, inv_ref[...], preferred_element_type=F32)
    cross_ref[...] = (res[rows:] * (1.0 / length)).astype(BF16)
    row = lax.broadcasted_iota(jnp.int32, (chans, chans), 0)
    col = lax.broadcasted_iota(jnp.int32, (chans, chans), 1)
    gain = jnp.sum(jnp.where(row == col, skip_ref[...], 0.0), axis=1, keepdims=True)
    gains = jnp.concatenate([gain, gain], axis=0)
    scale = length**-0.5 / length
    both = (res[:rows] * scale + gains * x.astype(F32)).astype(BF16)
    for s in range(parts):
        back_ref[s] = both[:, s * pos : (s + 1) * pos]


def unpack_kernel(back_ref, grad_ref, val_ref, gate_ref):
    parts, rows, _ = back_ref.shape
    chans = rows // 2
    conv = jnp.concatenate([back_ref[s, :chans, :] for s in range(parts)], axis=0)
    vals = jnp.concatenate([back_ref[s, chans:, :] for s in range(parts)], axis=0)
    gate_ref[0] = (grad_ref[0].astype(F32) * conv.astype(F32).T).astype(BF16)
    val_ref[0] = vals.astype(F32).T.astype(BF16)


def sum_over_dp(part, count):
    terms = [part.astype(F32)] + [
        lax.ppermute(part, "dp", [(j, j ^ d) for j in range(count)]).astype(F32)
        for d in range(1, count)
    ]
    while len(terms) > 1:
        terms = [a + b for a, b in zip(terms[::2], terms[1::2])]
    return terms[0]


def per_device_short(values, gates, grad_out, filters, skip):
    chans, length = filters.shape
    parts = lax.axis_size("ctx")
    seqs = lax.axis_size("dp")
    _, pos, width = values.shape
    rows = 2 * chans
    high, low, inv = dense_tables(length)
    params = pltpu.CompilerParams(vmem_limit_bytes=VMEM_BYTES)
    sent = pl.pallas_call(
        functools.partial(pack_kernel, parts),
        out_shape=jax.ShapeDtypeStruct((parts, rows, pos), BF16),
        in_specs=vmem_specs(3),
        out_specs=vmem_specs(1)[0],
        compiler_params=params,
        name="pack",
    )(values, gates, grad_out)
    held = lax.all_to_all(sent, "ctx", split_axis=0, concat_axis=0, tiled=True)
    fwd = in_vmem(jnp.asarray(high))
    spec = pl.pallas_call(
        filter_kernel,
        out_shape=jax.ShapeDtypeStruct((chans, 2 * length), F32),
        in_specs=vmem_specs(3),
        out_specs=vmem_specs(1)[0],
        compiler_params=params,
        cost_estimate=pl.CostEstimate(
            flops=12 * chans * length * length, bytes_accessed=8 * length * length, transcendentals=0
        ),
        name="filter_spectrum",
    )(filters, fwd, in_vmem(jnp.asarray(low)))
    back, cross = pl.pallas_call(
        main_kernel,
        out_shape=(
            jax.ShapeDtypeStruct((parts, rows, pos), BF16),
            jax.ShapeDtypeStruct((chans, length), BF16),
        ),
        in_specs=vmem_specs(5),
        out_specs=tuple(vmem_specs(2)),
        compiler_params=params,
        name="products",
    )(held, fwd, in_vmem(jnp.asarray(inv)), in_vmem(spec), skip.reshape(1, chans))
    total = sum_over_dp(cross, seqs)
    home = lax.all_to_all(back, "ctx", split_axis=0, concat_axis=0, tiled=True)
    grad_values, grad_gates = pl.pallas_call(
        unpack_kernel,
        out_shape=(
            jax.ShapeDtypeStruct((1, pos, width), BF16),
            jax.ShapeDtypeStruct((1, pos, width), BF16),
        ),
        in_specs=vmem_specs(2),
        out_specs=tuple(vmem_specs(2)),
        compiler_params=params,
        name="unpack",
    )(home, grad_out)
    return (grad_values, grad_gates, (seqs * length) ** (-0.5) * total)


def per_device(values, gates, grad_out, filters, skip):
    seqs = lax.axis_size("dp")
    if filters.shape[1] <= DENSE_LIMIT and seqs & (seqs - 1) == 0:
        return per_device_short(values, gates, grad_out, filters, skip)
    return per_device_long(values, gates, grad_out, filters, skip)


def solution(mesh):
    in_specs = (
        P("dp", "ctx", None),
        P("dp", "ctx", None),
        P("dp", "ctx", None),
        P("ctx", None),
        P("ctx"),
    )
    out_specs = (P("dp", "ctx", None), P("dp", "ctx", None), P("ctx", None))
    return jax.shard_map(
        per_device, mesh=mesh, in_specs=in_specs, out_specs=out_specs, check_vma=False
    )
```

```python
import functools
import math

import jax
import jax.numpy as jnp
import numpy as np
from jax import lax
from jax.experimental import pallas as pl
from jax.experimental.pallas import tpu as pltpu
from jax.sharding import PartitionSpec as P

HIGH = lax.Precision.HIGHEST
BF16 = jnp.bfloat16
F32 = jnp.float32
DENSE_LIMIT = 1024
VMEM_BYTES = 16 * 2**20


def twiddle(rows, cols, period):
    left = lax.broadcasted_iota(jnp.int32, (rows, cols), 0)
    right = lax.broadcasted_iota(jnp.int32, (rows, cols), 1)
    angle = (left * right % period).astype(jnp.float32) * (2.0 * math.pi / period)
    return (jnp.cos(angle), jnp.sin(angle))


def pick_first(period):
    best = 2
    for cand in range(2, math.isqrt(period) + 1):
        if period % cand == 0 and cand % 2 == 0:
            best = cand
    return best


def make_tables(length):
    period = 2 * length
    first = pick_first(period)
    second = period // first
    half = first // 2
    return (
        twiddle(half, first, first),
        twiddle(first, second, period),
        twiddle(second, second, second),
        half,
        first,
        second,
        period,
    )


def forward(signal, tables):
    (cos_one, sin_one), (cos_mid, sin_mid), (cos_two, sin_two), half, first, second, period = tables
    shaped = signal.reshape(signal.shape[0], half, second)
    part_re = jnp.einsum("cmn,mk->ckn", shaped, cos_one, precision=HIGH)
    part_im = -jnp.einsum("cmn,mk->ckn", shaped, sin_one, precision=HIGH)
    mid_re = part_re * cos_mid + part_im * sin_mid
    mid_im = part_im * cos_mid - part_re * sin_mid
    spec_re = jnp.einsum("ckn,nm->ckm", mid_re, cos_two, precision=HIGH) + jnp.einsum(
        "ckn,nm->ckm", mid_im, sin_two, precision=HIGH
    )
    spec_im = jnp.einsum("ckn,nm->ckm", mid_im, cos_two, precision=HIGH) - jnp.einsum(
        "ckn,nm->ckm", mid_re, sin_two, precision=HIGH
    )
    return (spec_re, spec_im)


def inverse(spec_re, spec_im, tables):
    (cos_one, sin_one), (cos_mid, sin_mid), (cos_two, sin_two), half, first, second, period = tables
    back_re = jnp.einsum("ckm,nm->ckn", spec_re, cos_two, precision=HIGH) - jnp.einsum(
        "ckm,nm->ckn", spec_im, sin_two, precision=HIGH
    )
    back_im = jnp.einsum("ckm,nm->ckn", spec_im, cos_two, precision=HIGH) + jnp.einsum(
        "ckm,nm->ckn", spec_re, sin_two, precision=HIGH
    )
    turned_re = back_re * cos_mid - back_im * sin_mid
    turned_im = back_im * cos_mid + back_re * sin_mid
    result = jnp.einsum("ckn,mk->cmn", turned_re, cos_one, precision=HIGH) - jnp.einsum(
        "ckn,mk->cmn", turned_im, sin_one, precision=HIGH
    )
    return result.reshape(spec_re.shape[0], half * second) * (1.0 / period)


def spectral(vals_f, dz_f, filt, gains, tables, scale_a):
    vals_re, vals_im = forward(vals_f, tables)
    dz_re, dz_im = forward(dz_f, tables)
    filt_re, filt_im = forward(filt, tables)
    conv_raw = inverse(
        filt_re * vals_re - filt_im * vals_im, filt_re * vals_im + filt_im * vals_re, tables
    )
    conv = (scale_a * conv_raw + gains * vals_f).astype(BF16)
    corr = inverse(filt_re * dz_re + filt_im * dz_im, filt_re * dz_im - filt_im * dz_re, tables)
    grad_val = (scale_a * corr + gains * dz_f).astype(BF16)
    cross = inverse(vals_re * dz_re + vals_im * dz_im, vals_re * dz_im - vals_im * dz_re, tables)
    return (grad_val, conv, cross)


def per_device_long(values, gates, grad_out, filters, skip):
    length = filters.shape[1]
    scale_a = length ** (-0.5)
    scale_b = (lax.axis_size("dp") * length) ** (-0.5)
    tok_grad = grad_out[0].astype(F32)
    dz_tok = (tok_grad * gates[0].astype(F32)).astype(BF16)
    vals_ch, dz_ch = (
        lax.all_to_all(values[0].T, "ctx", split_axis=0, concat_axis=1, tiled=True),
        lax.all_to_all(dz_tok.T, "ctx", split_axis=0, concat_axis=1, tiled=True),
    )
    grad_val, conv, cross = spectral(
        vals_ch.astype(F32),
        dz_ch.astype(F32),
        filters,
        skip[:, None],
        make_tables(length),
        scale_a,
    )
    total = lax.psum(cross, "dp")
    val_back, conv_back = (
        lax.all_to_all(grad_val, "ctx", split_axis=1, concat_axis=0, tiled=True),
        lax.all_to_all(conv, "ctx", split_axis=1, concat_axis=0, tiled=True),
    )
    grad_gate_tok = (tok_grad * conv_back.T.astype(F32)).astype(BF16)
    return (val_back.T[None], grad_gate_tok[None], scale_b * total)


def dense_tables(half):
    n = np.arange(half, dtype=np.int64)[:, None]
    k = np.concatenate([np.arange(0, half, 2), np.arange(1, half, 2)])[None, :]
    angle = ((2 * k + 1) * n % (4 * half)).astype(np.float64) * (math.pi / (2 * half))
    full = np.concatenate([np.cos(angle), -np.sin(angle)], axis=1).astype(BF16)
    return full, np.ascontiguousarray(full.T)


def vmem_specs(count):
    return [pl.BlockSpec(memory_space=pltpu.VMEM)] * count


def hbm_specs(count):
    return [pl.BlockSpec(memory_space=pltpu.HBM)] * count


def in_vmem(array):
    return pltpu.with_memory_space_constraint(array, pltpu.VMEM)


def in_hbm(array):
    return pltpu.with_memory_space_constraint(array, pltpu.HBM)


def start_copies(pairs, sems):
    copies = [pltpu.make_async_copy(a, b, sems.at[i]) for i, (a, b) in enumerate(pairs)]
    for copy in copies:
        copy.start()
    return copies


def pack_kernel(parts, vals_hbm, gate_hbm, grad_hbm, out_ref, grad_ref, vals_ref, gate_ref, sems):
    chans = vals_ref.shape[2] // parts
    copies = start_copies(
        [(vals_hbm, vals_ref), (gate_hbm, gate_ref), (grad_hbm, grad_ref)], sems
    )
    copies[0].wait()
    vals = vals_ref[0].astype(F32).T.astype(BF16)
    for d in range(parts):
        out_ref[d, :chans, :] = vals[d * chans : (d + 1) * chans, :]
    copies[1].wait()
    copies[2].wait()
    dz = (grad_ref[0].astype(F32) * gate_ref[0].astype(F32)).T.astype(BF16)
    for d in range(parts):
        out_ref[d, chans:, :] = dz[d * chans : (d + 1) * chans, :]


def filter_kernel(filt_hbm, fwd_hbm, inv_hbm, spec_ref, fwd_ref, inv_ref, filt_ref, sems):
    copies = start_copies([(filt_hbm, filt_ref), (fwd_hbm, fwd_ref), (inv_hbm, inv_ref)], sems)
    half = fwd_ref.shape[0]
    copies[0].wait()
    filt = jnp.concatenate([filt_ref[:, :half], filt_ref[:, half:]], axis=0)
    high = filt.astype(BF16)
    low = (filt - high.astype(F32)).astype(BF16)
    copies[1].wait()
    both = jnp.dot(
        jnp.concatenate([high, low], axis=0), fwd_ref[...], preferred_element_type=F32
    )
    spec_ref[...] = both[: filt.shape[0]] + both[filt.shape[0] :]
    copies[2].wait()


def mul(a, b):
    return (a[0] * b[0] - a[1] * b[1], a[0] * b[1] + a[1] * b[0])


def conj_mul(a, b):
    return (a[0] * b[0] + a[1] * b[1], a[0] * b[1] - a[1] * b[0])


def add(a, b):
    return (a[0] + b[0], a[1] + b[1])


def later(a, odd):
    return (a[1], -a[0]) if odd else (-a[1], a[0])


def main_kernel(
    x_ref, fwd_ref, inv_ref, filt_ref, skip_ref, back_ref, cross_ref, spec_ref, prod_ref
):
    parts, rows, pos = x_ref.shape
    chans = rows // 2
    half = parts // 2 * pos
    x = [
        jnp.concatenate([x_ref[s] for s in range(parts // 2)], axis=1),
        jnp.concatenate([x_ref[s] for s in range(parts // 2, parts)], axis=1),
    ]
    spec_ref[...] = jnp.dot(
        jnp.concatenate(x, axis=0), fwd_ref[...], preferred_element_type=F32
    )
    for r in range(0, chans, 16):
        for c in range(0, half, 128):
            odd = c >= half // 2

            def load(ref, row):
                at = slice(row + r, row + r + 16)
                return (ref[at, c : c + 128], ref[at, half + c : half + c + 128])

            v0, g0, v1, g1 = [load(spec_ref, i * chans) for i in range(4)]
            h0, h1 = [load(filt_ref, i * chans) for i in range(2)]
            conv0 = mul(h0, v0)
            conv1 = add(add(mul(h0, v1), mul(h1, v0)), later(conv0, odd))
            corr1 = conj_mul(h0, g1)
            corr0 = add(add(conj_mul(h0, g0), conj_mul(h1, g1)), later(corr1, not odd))
            cross1 = conj_mul(v0, g1)
            cross0 = add(add(conj_mul(v0, g0), conj_mul(v1, g1)), later(cross1, not odd))
            for i, (re, im) in enumerate((conv0, corr0, cross0, conv1, corr1, cross1)):
                at = slice(i * chans + r, i * chans + r + 16)
                prod_ref[at, c : c + 128] = re.astype(BF16)
                prod_ref[at, half + c : half + c + 128] = im.astype(BF16)
    res = jnp.dot(prod_ref[...], inv_ref[...], preferred_element_type=F32)
    row = lax.broadcasted_iota(jnp.int32, (chans, chans), 0)
    col = lax.broadcasted_iota(jnp.int32, (chans, chans), 1)
    gain = jnp.sum(jnp.where(row == col, skip_ref[...], 0.0), axis=1, keepdims=True)
    gains = jnp.concatenate([gain, gain], axis=0)
    scale = (2 * half) ** -0.5 / half
    for i in range(2):
        top = i * 3 * chans
        cross_ref[:, i * half : (i + 1) * half] = (
            res[top + rows : top + rows + chans] * (1.0 / half)
        ).astype(BF16)
        both = (res[top : top + rows] * scale + gains * x[i].astype(F32)).astype(BF16)
        for s in range(parts // 2):
            back_ref[i * (parts // 2) + s] = both[:, s * pos : (s + 1) * pos]


def unpack_kernel(back_ref, grad_ref, val_hbm, gate_hbm, val_ref, gate_ref, sems):
    parts, rows, _ = back_ref.shape
    chans = rows // 2
    vals = jnp.concatenate([back_ref[s, chans:, :] for s in range(parts)], axis=0)
    val_ref[0] = vals.astype(F32).T.astype(BF16)
    first = start_copies([(val_ref, val_hbm)], sems)
    conv = jnp.concatenate([back_ref[s, :chans, :] for s in range(parts)], axis=0)
    gate_ref[0] = (grad_ref[0].astype(F32) * conv.astype(F32).T).astype(BF16)
    second = pltpu.make_async_copy(gate_ref, gate_hbm, sems.at[1])
    second.start()
    first[0].wait()
    second.wait()


def total_kernel(scale, *refs):
    part_refs, out_hbm, out_ref, sems = refs[:-3], refs[-3], refs[-2], refs[-1]
    half = out_ref.shape[0] // 2
    copies = []
    for i in range(2):
        at = pl.ds(i * half, half)
        terms = [ref[at, :].astype(F32) for ref in part_refs]
        while len(terms) > 1:
            terms = [a + b for a, b in zip(terms[::2], terms[1::2])]
        out_ref[at, :] = terms[0] * scale
        copies.append(pltpu.make_async_copy(out_ref.at[at, :], out_hbm.at[at, :], sems.at[i]))
        copies[-1].start()
    for copy in copies:
        copy.wait()


def call(kernel, name, outs, ins, in_specs, scratch=(), sems=0, flops=0, moved=0):
    return pl.pallas_call(
        kernel,
        out_shape=tuple(
            pltpu.VMEM(shape, dtype) if near else jax.ShapeDtypeStruct(shape, dtype)
            for shape, dtype, near in outs
        ),
        in_specs=in_specs,
        out_specs=tuple(vmem_specs(1)[0] if near else hbm_specs(1)[0] for _, _, near in outs),
        scratch_shapes=[pltpu.VMEM(s, t) for s, t in scratch]
        + ([pltpu.SemaphoreType.DMA((sems,))] if sems else []),
        compiler_params=pltpu.CompilerParams(vmem_limit_bytes=VMEM_BYTES),
        cost_estimate=pl.CostEstimate(flops=flops, bytes_accessed=moved, transcendentals=0),
        name=name,
    )(*ins)


def per_device_short(values, gates, grad_out, filters, skip):
    chans, length = filters.shape
    parts = lax.axis_size("ctx")
    seqs = lax.axis_size("dp")
    _, pos, width = values.shape
    rows = 2 * chans
    fwd, inv = (jnp.asarray(table) for table in dense_tables(length // 2))
    token = ((1, pos, width), BF16)
    sent, grad_near = call(
        functools.partial(pack_kernel, parts),
        "pack",
        [((parts, rows, pos), BF16, True), (*token, True)],
        tuple(in_hbm(x) for x in (values, gates, grad_out)),
        hbm_specs(3),
        scratch=[token, token],
        sems=3,
        moved=8 * pos * width,
    )
    held = lax.all_to_all(sent, "ctx", split_axis=0, concat_axis=0, tiled=True)
    spec, fwd_near, inv_near = call(
        filter_kernel,
        "filter_spectrum",
        [((rows, length), F32, True), (fwd.shape, BF16, True), (inv.shape, BF16, True)],
        tuple(in_hbm(x) for x in (filters, fwd, inv)),
        hbm_specs(3),
        scratch=[((chans, length), F32)],
        sems=3,
        flops=4 * chans * length * length,
        moved=8 * length * length,
    )
    back, cross = call(
        main_kernel,
        "products",
        [((parts, rows, pos), BF16, True), ((chans, length), BF16, True)],
        (in_vmem(held), in_vmem(fwd_near), in_vmem(inv_near), in_vmem(spec), skip.reshape(1, chans)),
        vmem_specs(5),
        scratch=[((2 * rows, length), F32), ((3 * rows, length), BF16)],
        flops=10 * chans * length * length,
        moved=8 * length * length,
    )
    others = [
        lax.ppermute(cross, "dp", [(j, j ^ d) for j in range(seqs)]) for d in range(1, seqs)
    ]
    home = lax.all_to_all(back, "ctx", split_axis=0, concat_axis=0, tiled=True)
    grad_values, grad_gates = call(
        unpack_kernel,
        "unpack",
        [(*token, False), (*token, False)],
        (in_vmem(home), in_vmem(grad_near)),
        vmem_specs(2),
        scratch=[token, token],
        sems=2,
        moved=10 * pos * width,
    )
    (grad_filters,) = call(
        functools.partial(total_kernel, (seqs * length) ** (-0.5)),
        "total",
        [((chans, length), F32, False)],
        tuple(in_vmem(part) for part in [cross] + others),
        vmem_specs(seqs),
        scratch=[((chans, length), F32)],
        sems=2,
        moved=12 * chans * length,
    )
    return (grad_values, grad_gates, grad_filters)


def per_device(values, gates, grad_out, filters, skip):
    chans, length = filters.shape
    pos = values.shape[1]
    seqs = lax.axis_size("dp")
    dense = length <= DENSE_LIMIT and length % 512 == 0 and chans % 16 == 0 and pos % 128 == 0
    if dense and seqs & (seqs - 1) == 0:
        return per_device_short(values, gates, grad_out, filters, skip)
    return per_device_long(values, gates, grad_out, filters, skip)


def solution(mesh):
    in_specs = (
        P("dp", "ctx", None),
        P("dp", "ctx", None),
        P("dp", "ctx", None),
        P("ctx", None),
        P("ctx"),
    )
    out_specs = (P("dp", "ctx", None), P("dp", "ctx", None), P("ctx", None))
    return jax.shard_map(
        per_device, mesh=mesh, in_specs=in_specs, out_specs=out_specs, check_vma=False
    )
```

```python
import functools
import math

import jax
import jax.numpy as jnp
import numpy as np
from jax import lax
from jax.experimental import pallas as pl
from jax.experimental.pallas import tpu as pltpu
from jax.sharding import PartitionSpec as P

HIGH = lax.Precision.HIGHEST
BF16 = jnp.bfloat16
F32 = jnp.float32
DENSE_LIMIT = 1024
VMEM_BYTES = 16 * 2**20


def twiddle(rows, cols, period):
    left = lax.broadcasted_iota(jnp.int32, (rows, cols), 0)
    right = lax.broadcasted_iota(jnp.int32, (rows, cols), 1)
    angle = (left * right % period).astype(jnp.float32) * (2.0 * math.pi / period)
    return (jnp.cos(angle), jnp.sin(angle))


def pick_first(period):
    best = 2
    for cand in range(2, math.isqrt(period) + 1):
        if period % cand == 0 and cand % 2 == 0:
            best = cand
    return best


def make_tables(length):
    period = 2 * length
    first = pick_first(period)
    second = period // first
    half = first // 2
    return (
        twiddle(half, first, first),
        twiddle(first, second, period),
        twiddle(second, second, second),
        half,
        first,
        second,
        period,
    )


def forward(signal, tables):
    (cos_one, sin_one), (cos_mid, sin_mid), (cos_two, sin_two), half, first, second, period = tables
    shaped = signal.reshape(signal.shape[0], half, second)
    part_re = jnp.einsum("cmn,mk->ckn", shaped, cos_one, precision=HIGH)
    part_im = -jnp.einsum("cmn,mk->ckn", shaped, sin_one, precision=HIGH)
    mid_re = part_re * cos_mid + part_im * sin_mid
    mid_im = part_im * cos_mid - part_re * sin_mid
    spec_re = jnp.einsum("ckn,nm->ckm", mid_re, cos_two, precision=HIGH) + jnp.einsum(
        "ckn,nm->ckm", mid_im, sin_two, precision=HIGH
    )
    spec_im = jnp.einsum("ckn,nm->ckm", mid_im, cos_two, precision=HIGH) - jnp.einsum(
        "ckn,nm->ckm", mid_re, sin_two, precision=HIGH
    )
    return (spec_re, spec_im)


def inverse(spec_re, spec_im, tables):
    (cos_one, sin_one), (cos_mid, sin_mid), (cos_two, sin_two), half, first, second, period = tables
    back_re = jnp.einsum("ckm,nm->ckn", spec_re, cos_two, precision=HIGH) - jnp.einsum(
        "ckm,nm->ckn", spec_im, sin_two, precision=HIGH
    )
    back_im = jnp.einsum("ckm,nm->ckn", spec_im, cos_two, precision=HIGH) + jnp.einsum(
        "ckm,nm->ckn", spec_re, sin_two, precision=HIGH
    )
    turned_re = back_re * cos_mid - back_im * sin_mid
    turned_im = back_im * cos_mid + back_re * sin_mid
    result = jnp.einsum("ckn,mk->cmn", turned_re, cos_one, precision=HIGH) - jnp.einsum(
        "ckn,mk->cmn", turned_im, sin_one, precision=HIGH
    )
    return result.reshape(spec_re.shape[0], half * second) * (1.0 / period)


def spectral(vals_f, dz_f, filt, gains, tables, scale_a):
    vals_re, vals_im = forward(vals_f, tables)
    dz_re, dz_im = forward(dz_f, tables)
    filt_re, filt_im = forward(filt, tables)
    conv_raw = inverse(
        filt_re * vals_re - filt_im * vals_im, filt_re * vals_im + filt_im * vals_re, tables
    )
    conv = (scale_a * conv_raw + gains * vals_f).astype(BF16)
    corr = inverse(filt_re * dz_re + filt_im * dz_im, filt_re * dz_im - filt_im * dz_re, tables)
    grad_val = (scale_a * corr + gains * dz_f).astype(BF16)
    cross = inverse(vals_re * dz_re + vals_im * dz_im, vals_re * dz_im - vals_im * dz_re, tables)
    return (grad_val, conv, cross)


def per_device_long(values, gates, grad_out, filters, skip):
    length = filters.shape[1]
    scale_a = length ** (-0.5)
    scale_b = (lax.axis_size("dp") * length) ** (-0.5)
    tok_grad = grad_out[0].astype(F32)
    dz_tok = (tok_grad * gates[0].astype(F32)).astype(BF16)
    vals_ch, dz_ch = (
        lax.all_to_all(values[0].T, "ctx", split_axis=0, concat_axis=1, tiled=True),
        lax.all_to_all(dz_tok.T, "ctx", split_axis=0, concat_axis=1, tiled=True),
    )
    grad_val, conv, cross = spectral(
        vals_ch.astype(F32),
        dz_ch.astype(F32),
        filters,
        skip[:, None],
        make_tables(length),
        scale_a,
    )
    total = lax.psum(cross, "dp")
    val_back, conv_back = (
        lax.all_to_all(grad_val, "ctx", split_axis=1, concat_axis=0, tiled=True),
        lax.all_to_all(conv, "ctx", split_axis=1, concat_axis=0, tiled=True),
    )
    grad_gate_tok = (tok_grad * conv_back.T.astype(F32)).astype(BF16)
    return (val_back.T[None], grad_gate_tok[None], scale_b * total)


def dense_tables(half):
    n = np.arange(half, dtype=np.int64)[:, None]
    k = np.concatenate([np.arange(0, half, 2), np.arange(1, half, 2)])[None, :]
    angle = ((2 * k + 1) * n % (4 * half)).astype(np.float64) * (math.pi / (2 * half))
    full = np.concatenate([np.cos(angle), -np.sin(angle)], axis=1).astype(BF16)
    return full, np.ascontiguousarray(full.T)


def vmem_specs(count):
    return [pl.BlockSpec(memory_space=pltpu.VMEM)] * count


def hbm_specs(count):
    return [pl.BlockSpec(memory_space=pl.ANY)] * count


def in_vmem(array):
    return pltpu.with_memory_space_constraint(array, pltpu.VMEM)


def in_hbm(array):
    return pltpu.with_memory_space_constraint(array, pltpu.HBM)


def start_copies(pairs, sems):
    copies = [pltpu.make_async_copy(a, b, sems.at[i]) for i, (a, b) in enumerate(pairs)]
    for copy in copies:
        copy.start()
    return copies


def places(parts):
    me = lax.axis_index("ctx")
    return [
        (f, d, 2 * ((me // 2) ^ d) + ((me % 2) ^ f)) for f in range(2) for d in range(parts // 2)
    ]


def pack_kernel(
    vals_hbm, gate_hbm, grad_hbm, own_ref, sib_ref, grad_ref, vals_ref, gate_ref, turn_ref, sems
):
    pairs, rows, _ = own_ref.shape
    chans = rows // 2
    copies = start_copies(
        [(vals_hbm, vals_ref), (gate_hbm, gate_ref), (grad_hbm, grad_ref)], sems
    )
    copies[0].wait()
    turn_ref[0] = vals_ref[0].astype(F32).T.astype(BF16)
    copies[1].wait()
    copies[2].wait()
    turn_ref[1] = (grad_ref[0].astype(F32) * gate_ref[0].astype(F32)).T.astype(BF16)
    for f, d, at in places(2 * pairs):
        out_ref = sib_ref if f else own_ref
        at = pl.multiple_of(at * chans, chans)
        out_ref[d, :chans, :] = turn_ref[0, pl.ds(at, chans), :]
        out_ref[d, chans:, :] = turn_ref[1, pl.ds(at, chans), :]


def merge_kernel(own_ref, got_ref, *out_refs):
    for d, out_ref in enumerate(out_refs, 1):
        out_ref[0] = own_ref[d]
        out_ref[1] = got_ref[d]


def arrived(own_ref, got_ref, *pair_refs):
    return lambda f, d: pair_refs[d - 1][f] if d else (got_ref if f else own_ref)[0]


def filter_kernel(
    filt_hbm, fwd_hbm, inv_hbm, skip_ref, spec_ref, fwd_ref, inv_ref, gain_ref, filt_ref, sems
):
    copies = start_copies([(filt_hbm, filt_ref), (fwd_hbm, fwd_ref), (inv_hbm, inv_ref)], sems)
    half = fwd_ref.shape[0]
    copies[0].wait()
    filt = jnp.concatenate([filt_ref[:, :half], filt_ref[:, half:]], axis=0)
    high = filt.astype(BF16)
    low = (filt - high.astype(F32)).astype(BF16)
    copies[1].wait()
    both = jnp.dot(
        jnp.concatenate([high, low], axis=0), fwd_ref[...], preferred_element_type=F32
    )
    spec_ref[...] = both[: filt.shape[0]] + both[filt.shape[0] :]
    chans = filt_ref.shape[0]
    row = lax.broadcasted_iota(jnp.int32, (chans, chans), 0)
    col = lax.broadcasted_iota(jnp.int32, (chans, chans), 1)
    gain = jnp.sum(jnp.where(row == col, skip_ref[...], 0.0), axis=1, keepdims=True)
    gain_ref[...] = jnp.broadcast_to(jnp.concatenate([gain, gain], axis=0), gain_ref.shape)
    copies[2].wait()


def mul(a, b):
    return (a[0] * b[0] - a[1] * b[1], a[0] * b[1] + a[1] * b[0])


def conj_mul(a, b):
    return (a[0] * b[0] + a[1] * b[1], a[0] * b[1] - a[1] * b[0])


def add(a, b):
    return (a[0] + b[0], a[1] + b[1])


def later(a, odd):
    return (a[1], -a[0]) if odd else (-a[1], a[0])


def main_kernel(pairs, *refs):
    fwd_ref, inv_ref, filt_ref, gain_ref = refs[pairs + 1 : pairs + 5]
    own_ref, sib_ref, cross_ref, spec_ref, prod_ref, block_ref = refs[pairs + 5 :]
    parts, rows, pos = block_ref.shape
    chans = rows // 2
    half = parts // 2 * pos
    block = arrived(*refs[: pairs + 1])
    for f, d, at in places(parts):
        block_ref[at] = block(f, d)
    x = [
        jnp.concatenate([block_ref[s] for s in range(parts // 2)], axis=1),
        jnp.concatenate([block_ref[s] for s in range(parts // 2, parts)], axis=1),
    ]
    spec_ref[...] = jnp.dot(
        jnp.concatenate(x, axis=0), fwd_ref[...], preferred_element_type=F32
    )
    for r in range(0, chans, 16):
        for c in range(0, half, 128):
            odd = c >= half // 2

            def load(ref, row):
                at = slice(row + r, row + r + 16)
                return (ref[at, c : c + 128], ref[at, half + c : half + c + 128])

            v0, g0, v1, g1 = [load(spec_ref, i * chans) for i in range(4)]
            h0, h1 = [load(filt_ref, i * chans) for i in range(2)]
            conv0 = mul(h0, v0)
            conv1 = add(add(mul(h0, v1), mul(h1, v0)), later(conv0, odd))
            corr1 = conj_mul(h0, g1)
            corr0 = add(add(conj_mul(h0, g0), conj_mul(h1, g1)), later(corr1, not odd))
            cross1 = conj_mul(v0, g1)
            cross0 = add(add(conj_mul(v0, g0), conj_mul(v1, g1)), later(cross1, not odd))
            for i, (re, im) in enumerate((conv0, corr0, cross0, conv1, corr1, cross1)):
                at = slice(i * chans + r, i * chans + r + 16)
                prod_ref[at, c : c + 128] = re.astype(BF16)
                prod_ref[at, half + c : half + c + 128] = im.astype(BF16)
    res = jnp.dot(prod_ref[...], inv_ref[...], preferred_element_type=F32)
    gains = jnp.concatenate([gain_ref[...]] * (half // 128), axis=1)
    scale = (2 * half) ** -0.5 / half
    for i in range(2):
        top = i * 3 * chans
        cross_ref[:, i * half : (i + 1) * half] = (
            res[top + rows : top + rows + chans] * (1.0 / half)
        ).astype(BF16)
        both = (res[top : top + rows] * scale + gains * x[i].astype(F32)).astype(BF16)
        for s in range(parts // 2):
            block_ref[i * (parts // 2) + s] = both[:, s * pos : (s + 1) * pos]
    for f, d, at in places(parts):
        (sib_ref if f else own_ref)[d] = block_ref[at]


def unpack_kernel(pairs, *refs):
    grad_ref, val_hbm, gate_hbm, val_ref, gate_ref, turn_ref, sems = refs[pairs + 1 :]
    chans = turn_ref.shape[1] // (2 * pairs)
    block = arrived(*refs[: pairs + 1])
    for f, d, at in places(2 * pairs):
        at = pl.multiple_of(at * chans, chans)
        both = block(f, d)
        turn_ref[0, pl.ds(at, chans), :] = both[:chans]
        turn_ref[1, pl.ds(at, chans), :] = both[chans:]
    val_ref[0] = turn_ref[1].astype(F32).T.astype(BF16)
    first = start_copies([(val_ref, val_hbm)], sems)
    gate_ref[0] = (grad_ref[0].astype(F32) * turn_ref[0].astype(F32).T).astype(BF16)
    second = pltpu.make_async_copy(gate_ref, gate_hbm, sems.at[1])
    second.start()
    first[0].wait()
    second.wait()


def pair_kernel(left_ref, right_ref, *rest):
    out_ref = rest[-1]
    out_ref[...] = (left_ref[...].astype(F32) + right_ref[...].astype(F32)).astype(BF16)


def total_kernel(scale, left_ref, right_ref, out_hbm, out_ref, sems):
    half = out_ref.shape[0] // 2
    copies = []
    for i in range(2):
        at = pl.ds(i * half, half)
        out_ref[at, :] = (left_ref[at, :].astype(F32) + right_ref[at, :].astype(F32)) * scale
        copies.append(pltpu.make_async_copy(out_ref.at[at, :], out_hbm.at[at, :], sems.at[i]))
        copies[-1].start()
    for copy in copies:
        copy.wait()


def call(kernel, name, outs, ins, in_specs, scratch=(), sems=0, flops=0, moved=0):
    return pl.pallas_call(
        kernel,
        out_shape=tuple(
            pltpu.VMEM(shape, dtype) if near else jax.ShapeDtypeStruct(shape, dtype)
            for shape, dtype, near in outs
        ),
        in_specs=in_specs,
        out_specs=tuple(vmem_specs(1)[0] if near else hbm_specs(1)[0] for _, _, near in outs),
        scratch_shapes=[pltpu.VMEM(s, t) for s, t in scratch]
        + ([pltpu.SemaphoreType.DMA((sems,))] if sems else []),
        compiler_params=pltpu.CompilerParams(vmem_limit_bytes=VMEM_BYTES),
        cost_estimate=pl.CostEstimate(flops=flops, bytes_accessed=moved, transcendentals=0),
        name=name,
    )(*ins)


def exchange(own, sib, name):
    pairs, rows, pos = own.shape
    got = lax.ppermute(sib, "ctx", [(j, j ^ 1) for j in range(2 * pairs)])
    sent = call(
        merge_kernel,
        "merge_" + name,
        [((2, rows, pos), BF16, True)] * (pairs - 1),
        (in_vmem(own), in_vmem(got)),
        vmem_specs(2),
        moved=8 * (pairs - 1) * rows * pos,
    )
    pair_of = [(d, [(j, j ^ (2 * d)) for j in range(2 * pairs)]) for d in range(1, pairs)]
    return [own, got] + [lax.ppermute(sent[d - 1], "ctx", perm) for d, perm in pair_of]


def per_device_short(values, gates, grad_out, filters, skip):
    chans, length = filters.shape
    parts = lax.axis_size("ctx")
    seqs = lax.axis_size("dp")
    _, pos, width = values.shape
    rows = 2 * chans
    fwd, inv = (jnp.asarray(table) for table in dense_tables(length // 2))
    token = ((1, pos, width), BF16)
    pairs = parts // 2
    pair_blocks = ((pairs, rows, pos), BF16)
    turned = ((2, width, pos), BF16)
    own, sib, grad_near = call(
        pack_kernel,
        "pack",
        [(*pair_blocks, True), (*pair_blocks, True), (*token, True)],
        tuple(in_hbm(x) for x in (values, gates, grad_out)),
        hbm_specs(3),
        scratch=[token, token, turned],
        sems=3,
        moved=8 * pos * width,
    )
    held = exchange(own, sib, "out")
    spec, fwd_near, inv_near, gains = call(
        filter_kernel,
        "filter_spectrum",
        [((rows, length), F32, True), (fwd.shape, BF16, True), (inv.shape, BF16, True), ((rows, 128), F32, True)],
        tuple(in_hbm(x) for x in (filters, fwd, inv)) + (skip.reshape(1, chans),),
        hbm_specs(3) + vmem_specs(1),
        scratch=[((chans, length), F32)],
        sems=3,
        flops=4 * chans * length * length,
        moved=8 * length * length,
    )
    own, sib, cross = call(
        functools.partial(main_kernel, pairs),
        "products",
        [(*pair_blocks, True), (*pair_blocks, True), ((chans, length), BF16, True)],
        tuple(in_vmem(x) for x in held + [fwd_near, inv_near, spec, gains]),
        vmem_specs(pairs + 5),
        scratch=[
            ((2 * rows, length), F32),
            ((3 * rows, length), BF16),
            ((parts, rows, pos), BF16),
        ],
        flops=10 * chans * length * length,
        moved=8 * length * length,
    )
    home = exchange(own, sib, "home")
    step = seqs // 2
    while step:
        other = lax.ppermute(cross, "dp", [(j, j ^ step) for j in range(seqs)])
        step //= 2
        if step:
            (cross,) = call(
                pair_kernel,
                "pair_sum",
                [((chans, length), BF16, True)],
                (in_vmem(cross), in_vmem(other), *home[2:]),
                vmem_specs(2) + hbm_specs(len(home) - 2),
                moved=6 * chans * length,
            )
    grad_values, grad_gates = call(
        functools.partial(unpack_kernel, pairs),
        "unpack",
        [(*token, False), (*token, False)],
        tuple(in_vmem(x) for x in home + [grad_near]),
        vmem_specs(pairs + 2),
        scratch=[token, token, turned],
        sems=2,
        moved=10 * pos * width,
    )
    (grad_filters,) = call(
        functools.partial(total_kernel, (seqs * length) ** (-0.5)),
        "total",
        [((chans, length), F32, False)],
        (in_vmem(cross), in_vmem(other)),
        vmem_specs(2),
        scratch=[((chans, length), F32)],
        sems=2,
        moved=12 * chans * length,
    )
    return (grad_values, grad_gates, grad_filters)


def per_device(values, gates, grad_out, filters, skip):
    chans, length = filters.shape
    pos = values.shape[1]
    seqs = lax.axis_size("dp")
    dense = length <= DENSE_LIMIT and length % 512 == 0 and chans % 16 == 0 and pos % 128 == 0
    powers = all(n > 1 and n & (n - 1) == 0 for n in (seqs, lax.axis_size("ctx")))
    if dense and powers:
        return per_device_short(values, gates, grad_out, filters, skip)
    return per_device_long(values, gates, grad_out, filters, skip)


def solution(mesh):
    in_specs = (
        P("dp", "ctx", None),
        P("dp", "ctx", None),
        P("dp", "ctx", None),
        P("ctx", None),
        P("ctx"),
    )
    out_specs = (P("dp", "ctx", None), P("dp", "ctx", None), P("ctx", None))
    return jax.shard_map(
        per_device, mesh=mesh, in_specs=in_specs, out_specs=out_specs, check_vma=False
    )
```

```python
import functools
import math

import jax
import jax.numpy as jnp
import numpy as np
from jax import lax
from jax.experimental import pallas as pl
from jax.experimental.pallas import tpu as pltpu
from jax.sharding import PartitionSpec as P

HIGH = lax.Precision.HIGHEST
BF16 = jnp.bfloat16
F32 = jnp.float32
DENSE_LIMIT = 1024
VMEM_BYTES = 16 * 2**20


def twiddle(rows, cols, period):
    left = lax.broadcasted_iota(jnp.int32, (rows, cols), 0)
    right = lax.broadcasted_iota(jnp.int32, (rows, cols), 1)
    angle = (left * right % period).astype(jnp.float32) * (2.0 * math.pi / period)
    return (jnp.cos(angle), jnp.sin(angle))


def pick_first(period):
    best = 2
    for cand in range(2, math.isqrt(period) + 1):
        if period % cand == 0 and cand % 2 == 0:
            best = cand
    return best


def make_tables(length):
    period = 2 * length
    first = pick_first(period)
    second = period // first
    half = first // 2
    return (
        twiddle(half, first, first),
        twiddle(first, second, period),
        twiddle(second, second, second),
        half,
        first,
        second,
        period,
    )


def forward(signal, tables):
    (cos_one, sin_one), (cos_mid, sin_mid), (cos_two, sin_two), half, first, second, period = tables
    shaped = signal.reshape(signal.shape[0], half, second)
    part_re = jnp.einsum("cmn,mk->ckn", shaped, cos_one, precision=HIGH)
    part_im = -jnp.einsum("cmn,mk->ckn", shaped, sin_one, precision=HIGH)
    mid_re = part_re * cos_mid + part_im * sin_mid
    mid_im = part_im * cos_mid - part_re * sin_mid
    spec_re = jnp.einsum("ckn,nm->ckm", mid_re, cos_two, precision=HIGH) + jnp.einsum(
        "ckn,nm->ckm", mid_im, sin_two, precision=HIGH
    )
    spec_im = jnp.einsum("ckn,nm->ckm", mid_im, cos_two, precision=HIGH) - jnp.einsum(
        "ckn,nm->ckm", mid_re, sin_two, precision=HIGH
    )
    return (spec_re, spec_im)


def inverse(spec_re, spec_im, tables):
    (cos_one, sin_one), (cos_mid, sin_mid), (cos_two, sin_two), half, first, second, period = tables
    back_re = jnp.einsum("ckm,nm->ckn", spec_re, cos_two, precision=HIGH) - jnp.einsum(
        "ckm,nm->ckn", spec_im, sin_two, precision=HIGH
    )
    back_im = jnp.einsum("ckm,nm->ckn", spec_im, cos_two, precision=HIGH) + jnp.einsum(
        "ckm,nm->ckn", spec_re, sin_two, precision=HIGH
    )
    turned_re = back_re * cos_mid - back_im * sin_mid
    turned_im = back_im * cos_mid + back_re * sin_mid
    result = jnp.einsum("ckn,mk->cmn", turned_re, cos_one, precision=HIGH) - jnp.einsum(
        "ckn,mk->cmn", turned_im, sin_one, precision=HIGH
    )
    return result.reshape(spec_re.shape[0], half * second) * (1.0 / period)


def spectral(vals_f, dz_f, filt, gains, tables, scale_a):
    vals_re, vals_im = forward(vals_f, tables)
    dz_re, dz_im = forward(dz_f, tables)
    filt_re, filt_im = forward(filt, tables)
    conv_raw = inverse(
        filt_re * vals_re - filt_im * vals_im, filt_re * vals_im + filt_im * vals_re, tables
    )
    conv = (scale_a * conv_raw + gains * vals_f).astype(BF16)
    corr = inverse(filt_re * dz_re + filt_im * dz_im, filt_re * dz_im - filt_im * dz_re, tables)
    grad_val = (scale_a * corr + gains * dz_f).astype(BF16)
    cross = inverse(vals_re * dz_re + vals_im * dz_im, vals_re * dz_im - vals_im * dz_re, tables)
    return (grad_val, conv, cross)


def per_device_long(values, gates, grad_out, filters, skip):
    length = filters.shape[1]
    scale_a = length ** (-0.5)
    scale_b = (lax.axis_size("dp") * length) ** (-0.5)
    tok_grad = grad_out[0].astype(F32)
    dz_tok = (tok_grad * gates[0].astype(F32)).astype(BF16)
    vals_ch, dz_ch = (
        lax.all_to_all(values[0].T, "ctx", split_axis=0, concat_axis=1, tiled=True),
        lax.all_to_all(dz_tok.T, "ctx", split_axis=0, concat_axis=1, tiled=True),
    )
    grad_val, conv, cross = spectral(
        vals_ch.astype(F32),
        dz_ch.astype(F32),
        filters,
        skip[:, None],
        make_tables(length),
        scale_a,
    )
    total = lax.psum(cross, "dp")
    val_back, conv_back = (
        lax.all_to_all(grad_val, "ctx", split_axis=1, concat_axis=0, tiled=True),
        lax.all_to_all(conv, "ctx", split_axis=1, concat_axis=0, tiled=True),
    )
    grad_gate_tok = (tok_grad * conv_back.T.astype(F32)).astype(BF16)
    return (val_back.T[None], grad_gate_tok[None], scale_b * total)


def dense_tables(half):
    n = np.arange(half, dtype=np.int64)[:, None]
    k = np.concatenate([np.arange(0, half, 2), np.arange(1, half, 2)])[None, :]
    angle = ((2 * k + 1) * n % (4 * half)).astype(np.float64) * (math.pi / (2 * half))
    full = np.concatenate([np.cos(angle), -np.sin(angle)], axis=1).astype(BF16)
    return full, np.ascontiguousarray(full.T)


def vmem_specs(count):
    return [pl.BlockSpec(memory_space=pltpu.VMEM)] * count


def hbm_specs(count):
    return [pl.BlockSpec(memory_space=pl.ANY)] * count


def in_vmem(array):
    return pltpu.with_memory_space_constraint(array, pltpu.VMEM)


def in_hbm(array):
    return pltpu.with_memory_space_constraint(array, pltpu.HBM)


def start_copies(pairs, sems):
    copies = [pltpu.make_async_copy(a, b, sems.at[i]) for i, (a, b) in enumerate(pairs)]
    for copy in copies:
        copy.start()
    return copies


def places(parts):
    me = lax.axis_index("ctx")
    return [
        (f, d, 2 * ((me // 2) ^ d) + ((me % 2) ^ f)) for f in range(2) for d in range(parts // 2)
    ]


def pack_kernel(
    vals_hbm, gate_hbm, grad_hbm, own_ref, sib_ref, grad_ref, vals_ref, gate_ref, turn_ref, sems
):
    pairs, rows, _ = own_ref.shape
    chans = rows // 2
    copies = start_copies(
        [(vals_hbm, vals_ref), (gate_hbm, gate_ref), (grad_hbm, grad_ref)], sems
    )
    copies[0].wait()
    turn_ref[0] = vals_ref[0].astype(F32).T.astype(BF16)
    copies[1].wait()
    copies[2].wait()
    turn_ref[1] = (grad_ref[0].astype(F32) * gate_ref[0].astype(F32)).T.astype(BF16)
    for f, d, at in places(2 * pairs):
        out_ref = sib_ref if f else own_ref
        at = pl.multiple_of(at * chans, chans)
        out_ref[d, :chans, :] = turn_ref[0, pl.ds(at, chans), :]
        out_ref[d, chans:, :] = turn_ref[1, pl.ds(at, chans), :]


def merge_kernel(own_ref, got_ref, *out_refs):
    for d, out_ref in enumerate(out_refs, 1):
        out_ref[0] = own_ref[d]
        out_ref[1] = got_ref[d]


def arrived(own_ref, got_ref, *pair_refs):
    return lambda f, d: pair_refs[-d][f] if d else (got_ref if f else own_ref)[0]


def filter_kernel(
    filt_hbm, fwd_hbm, inv_hbm, skip_ref, spec_ref, fwd_ref, inv_ref, gain_ref, filt_ref, sems
):
    copies = start_copies([(filt_hbm, filt_ref), (fwd_hbm, fwd_ref), (inv_hbm, inv_ref)], sems)
    half = fwd_ref.shape[0]
    copies[0].wait()
    filt = jnp.concatenate([filt_ref[:, :half], filt_ref[:, half:]], axis=0)
    high = filt.astype(BF16)
    low = (filt - high.astype(F32)).astype(BF16)
    copies[1].wait()
    both = jnp.dot(
        jnp.concatenate([high, low], axis=0), fwd_ref[...], preferred_element_type=F32
    )
    spec_ref[...] = both[: filt.shape[0]] + both[filt.shape[0] :]
    chans = filt_ref.shape[0]
    row = lax.broadcasted_iota(jnp.int32, (chans, chans), 0)
    col = lax.broadcasted_iota(jnp.int32, (chans, chans), 1)
    gain = jnp.sum(jnp.where(row == col, skip_ref[...], 0.0), axis=1, keepdims=True)
    gain_ref[...] = jnp.broadcast_to(jnp.concatenate([gain, gain], axis=0), gain_ref.shape)
    copies[2].wait()


def mul(a, b):
    return (a[0] * b[0] - a[1] * b[1], a[0] * b[1] + a[1] * b[0])


def conj_mul(a, b):
    return (a[0] * b[0] + a[1] * b[1], a[0] * b[1] - a[1] * b[0])


def add(a, b):
    return (a[0] + b[0], a[1] + b[1])


def later(a, odd):
    return (a[1], -a[0]) if odd else (-a[1], a[0])


def main_kernel(pairs, *refs):
    fwd_ref, inv_ref, filt_ref, gain_ref = refs[pairs + 1 : pairs + 5]
    back_hbm, cross_ref, spec_ref, prod_ref, block_ref, back_ref, sems = refs[pairs + 5 :]
    parts, rows, pos = block_ref.shape
    chans = rows // 2
    half = parts // 2 * pos
    block = arrived(*refs[: pairs + 1])
    for f, d, at in places(parts):
        block_ref[at] = block(f, d)
    x = [
        jnp.concatenate([block_ref[s] for s in range(parts // 2)], axis=1),
        jnp.concatenate([block_ref[s] for s in range(parts // 2, parts)], axis=1),
    ]
    spec_ref[...] = jnp.dot(
        jnp.concatenate(x, axis=0), fwd_ref[...], preferred_element_type=F32
    )
    for r in range(0, chans, 16):
        for c in range(0, half, 128):
            odd = c >= half // 2

            def load(ref, row):
                at = slice(row + r, row + r + 16)
                return (ref[at, c : c + 128], ref[at, half + c : half + c + 128])

            v0, g0, v1, g1 = [load(spec_ref, i * chans) for i in range(4)]
            h0, h1 = [load(filt_ref, i * chans) for i in range(2)]
            conv0 = mul(h0, v0)
            conv1 = add(add(mul(h0, v1), mul(h1, v0)), later(conv0, odd))
            corr1 = conj_mul(h0, g1)
            corr0 = add(add(conj_mul(h0, g0), conj_mul(h1, g1)), later(corr1, not odd))
            cross1 = conj_mul(v0, g1)
            cross0 = add(add(conj_mul(v0, g0), conj_mul(v1, g1)), later(cross1, not odd))
            for i, (re, im) in enumerate((conv0, corr0, conv1, corr1, cross0, cross1)):
                at = slice(i * chans + r, i * chans + r + 16)
                prod_ref[at, c : c + 128] = re.astype(BF16)
                prod_ref[at, half + c : half + c + 128] = im.astype(BF16)
    inv = inv_ref[...]
    gains = jnp.concatenate([gain_ref[...]] * (half // 128), axis=1)
    scale = (2 * half) ** -0.5 / half
    copies = []
    res = jnp.dot(prod_ref[: 2 * rows], inv, preferred_element_type=F32) * scale
    for i in range(2):
        both = (res[i * rows : (i + 1) * rows] + gains * x[i].astype(F32)).astype(BF16)
        first = i * (parts // 2)
        for s in range(parts // 2):
            back_ref[first + s] = both[:, s * pos : (s + 1) * pos]
        at = pl.ds(first, parts // 2)
        copies += start_copies([(back_ref.at[at], back_hbm.at[at])], sems.at[pl.ds(i, 1)])
    res = jnp.dot(prod_ref[2 * rows :], inv, preferred_element_type=F32) * (1.0 / half)
    for i in range(2):
        cross_ref[:, i * half : (i + 1) * half] = res[i * chans : (i + 1) * chans].astype(BF16)
    for copy in copies:
        copy.wait()


def pair_kernel(left_ref, right_ref, out_ref):
    out_ref[...] = (left_ref[...].astype(F32) + right_ref[...].astype(F32)).astype(BF16)


def finish_kernel(
    scale,
    left_ref,
    right_ref,
    back_ref,
    near_ref,
    val_hbm,
    gate_hbm,
    filt_hbm,
    val_ref,
    gate_ref,
    filt_ref,
    sems,
):
    parts, rows, _ = back_ref.shape
    chans = rows // 2
    filt_ref[...] = (left_ref[...].astype(F32) + right_ref[...].astype(F32)) * scale
    copies = start_copies([(filt_ref, filt_hbm)], sems)
    vals = jnp.concatenate([back_ref[s, chans:, :] for s in range(parts)], axis=0)
    val_ref[0] = vals.astype(F32).T.astype(BF16)
    copies += start_copies([(val_ref, val_hbm)], sems.at[pl.ds(1, 1)])
    conv = jnp.concatenate([back_ref[s, :chans, :] for s in range(parts)], axis=0)
    gate_ref[0] = (near_ref[0].astype(F32) * conv.astype(F32).T).astype(BF16)
    copies += start_copies([(gate_ref, gate_hbm)], sems.at[pl.ds(2, 1)])
    for copy in copies:
        copy.wait()


def call(kernel, name, outs, ins, in_specs, scratch=(), sems=0, flops=0, moved=0):
    return pl.pallas_call(
        kernel,
        out_shape=tuple(
            pltpu.VMEM(shape, dtype) if near else jax.ShapeDtypeStruct(shape, dtype)
            for shape, dtype, near in outs
        ),
        in_specs=in_specs,
        out_specs=tuple(vmem_specs(1)[0] if near else hbm_specs(1)[0] for _, _, near in outs),
        scratch_shapes=[pltpu.VMEM(s, t) for s, t in scratch]
        + ([pltpu.SemaphoreType.DMA((sems,))] if sems else []),
        compiler_params=pltpu.CompilerParams(vmem_limit_bytes=VMEM_BYTES),
        cost_estimate=pl.CostEstimate(flops=flops, bytes_accessed=moved, transcendentals=0),
        name=name,
    )(*ins)


def exchange(own, sib, name):
    pairs, rows, pos = own.shape
    got = lax.ppermute(sib, "ctx", [(j, j ^ 1) for j in range(2 * pairs)])
    sent = call(
        merge_kernel,
        "merge_" + name,
        [((2, rows, pos), BF16, True)] * (pairs - 1),
        (in_vmem(own), in_vmem(got)),
        vmem_specs(2),
        moved=8 * (pairs - 1) * rows * pos,
    )
    held = [
        lax.ppermute(sent[d - 1], "ctx", [(j, j ^ (2 * d)) for j in range(2 * pairs)])
        for d in reversed(range(1, pairs))
    ]
    return [own, got] + held


def dp_pairs(seqs, parts, step):
    pairs = []
    for s in range(seqs):
        for c in range(parts):
            other = s ^ (seqs // 2 // step if c % 2 else step)
            pairs.append((s * parts + c, other * parts + c))
    return pairs


def per_device_short(values, gates, grad_out, filters, skip):
    chans, length = filters.shape
    parts = lax.axis_size("ctx")
    seqs = lax.axis_size("dp")
    _, pos, width = values.shape
    rows = 2 * chans
    fwd, inv = (jnp.asarray(table) for table in dense_tables(length // 2))
    token = ((1, pos, width), BF16)
    pairs = parts // 2
    pair_blocks = ((pairs, rows, pos), BF16)
    turned = ((2, width, pos), BF16)
    own, sib, grad_near = call(
        pack_kernel,
        "pack",
        [(*pair_blocks, True), (*pair_blocks, True), (*token, True)],
        tuple(in_hbm(x) for x in (values, gates, grad_out)),
        hbm_specs(3),
        scratch=[token, token, turned],
        sems=3,
        moved=8 * pos * width,
    )
    held = exchange(own, sib, "out")
    spec, fwd_near, inv_near, gains = call(
        filter_kernel,
        "filter_spectrum",
        [
            ((rows, length), F32, True),
            (fwd.shape, BF16, True),
            (inv.shape, BF16, True),
            ((rows, 128), F32, True),
        ],
        tuple(in_hbm(x) for x in (filters, fwd, inv)) + (skip.reshape(1, chans),),
        hbm_specs(3) + vmem_specs(1),
        scratch=[((chans, length), F32)],
        sems=3,
        flops=4 * chans * length * length,
        moved=8 * length * length,
    )
    back, cross = call(
        functools.partial(main_kernel, pairs),
        "products",
        [((parts, rows, pos), BF16, False), ((chans, length), BF16, True)],
        tuple(in_vmem(x) for x in held + [fwd_near, inv_near, spec, gains]),
        vmem_specs(pairs + 5),
        scratch=[
            ((2 * rows, length), F32),
            ((3 * rows, length), BF16),
            ((parts, rows, pos), BF16),
            ((parts, rows, pos), BF16),
        ],
        sems=2,
        flops=10 * chans * length * length,
        moved=8 * length * length,
    )
    home = lax.all_to_all(back, "ctx", split_axis=0, concat_axis=0, tiled=True)
    step = seqs // 2
    while step:
        other = lax.ppermute(cross, ("dp", "ctx"), dp_pairs(seqs, parts, step))
        step //= 2
        if step:
            (cross,) = call(
                pair_kernel,
                "pair_sum",
                [((chans, length), BF16, True)],
                (in_vmem(cross), in_vmem(other)),
                vmem_specs(2),
                moved=6 * chans * length,
            )
    grad_values, grad_gates, grad_filters = call(
        functools.partial(finish_kernel, (seqs * length) ** (-0.5)),
        "finish",
        [(*token, False), (*token, False), ((chans, length), F32, False)],
        tuple(in_vmem(x) for x in (cross, other, home, grad_near)),
        vmem_specs(4),
        scratch=[token, token, ((chans, length), F32)],
        sems=3,
        moved=10 * pos * width + 8 * chans * length,
    )
    return (grad_values, grad_gates, grad_filters)


def per_device(values, gates, grad_out, filters, skip):
    chans, length = filters.shape
    pos = values.shape[1]
    seqs = lax.axis_size("dp")
    dense = length <= DENSE_LIMIT and length % 512 == 0 and chans % 16 == 0 and pos % 128 == 0
    powers = all(n > 1 and n & (n - 1) == 0 for n in (seqs, lax.axis_size("ctx")))
    if dense and powers:
        return per_device_short(values, gates, grad_out, filters, skip)
    return per_device_long(values, gates, grad_out, filters, skip)


def solution(mesh):
    in_specs = (
        P("dp", "ctx", None),
        P("dp", "ctx", None),
        P("dp", "ctx", None),
        P("ctx", None),
        P("ctx"),
    )
    out_specs = (P("dp", "ctx", None), P("dp", "ctx", None), P("ctx", None))
    return jax.shard_map(
        per_device, mesh=mesh, in_specs=in_specs, out_specs=out_specs, check_vma=False
    )
```

```python
import functools
import math

import jax
import jax.numpy as jnp
import numpy as np
from jax import lax
from jax.experimental import pallas as pl
from jax.experimental.pallas import tpu as pltpu
from jax.sharding import PartitionSpec as P

HIGH = lax.Precision.HIGHEST
BF16 = jnp.bfloat16
F32 = jnp.float32
DENSE_LIMIT = 1024
VMEM_BYTES = 16 * 2**20


def twiddle(rows, cols, period):
    left = lax.broadcasted_iota(jnp.int32, (rows, cols), 0)
    right = lax.broadcasted_iota(jnp.int32, (rows, cols), 1)
    angle = (left * right % period).astype(jnp.float32) * (2.0 * math.pi / period)
    return (jnp.cos(angle), jnp.sin(angle))


def pick_first(period):
    best = 2
    for cand in range(2, math.isqrt(period) + 1):
        if period % cand == 0 and cand % 2 == 0:
            best = cand
    return best


def make_tables(length):
    period = 2 * length
    first = pick_first(period)
    second = period // first
    half = first // 2
    return (
        twiddle(half, first, first),
        twiddle(first, second, period),
        twiddle(second, second, second),
        half,
        first,
        second,
        period,
    )


def forward(signal, tables):
    (cos_one, sin_one), (cos_mid, sin_mid), (cos_two, sin_two), half, first, second, period = tables
    shaped = signal.reshape(signal.shape[0], half, second)
    part_re = jnp.einsum("cmn,mk->ckn", shaped, cos_one, precision=HIGH)
    part_im = -jnp.einsum("cmn,mk->ckn", shaped, sin_one, precision=HIGH)
    mid_re = part_re * cos_mid + part_im * sin_mid
    mid_im = part_im * cos_mid - part_re * sin_mid
    spec_re = jnp.einsum("ckn,nm->ckm", mid_re, cos_two, precision=HIGH) + jnp.einsum(
        "ckn,nm->ckm", mid_im, sin_two, precision=HIGH
    )
    spec_im = jnp.einsum("ckn,nm->ckm", mid_im, cos_two, precision=HIGH) - jnp.einsum(
        "ckn,nm->ckm", mid_re, sin_two, precision=HIGH
    )
    return (spec_re, spec_im)


def inverse(spec_re, spec_im, tables):
    (cos_one, sin_one), (cos_mid, sin_mid), (cos_two, sin_two), half, first, second, period = tables
    back_re = jnp.einsum("ckm,nm->ckn", spec_re, cos_two, precision=HIGH) - jnp.einsum(
        "ckm,nm->ckn", spec_im, sin_two, precision=HIGH
    )
    back_im = jnp.einsum("ckm,nm->ckn", spec_im, cos_two, precision=HIGH) + jnp.einsum(
        "ckm,nm->ckn", spec_re, sin_two, precision=HIGH
    )
    turned_re = back_re * cos_mid - back_im * sin_mid
    turned_im = back_im * cos_mid + back_re * sin_mid
    result = jnp.einsum("ckn,mk->cmn", turned_re, cos_one, precision=HIGH) - jnp.einsum(
        "ckn,mk->cmn", turned_im, sin_one, precision=HIGH
    )
    return result.reshape(spec_re.shape[0], half * second) * (1.0 / period)


def spectral(vals_f, dz_f, filt, gains, tables, scale_a):
    vals_re, vals_im = forward(vals_f, tables)
    dz_re, dz_im = forward(dz_f, tables)
    filt_re, filt_im = forward(filt, tables)
    conv_raw = inverse(
        filt_re * vals_re - filt_im * vals_im, filt_re * vals_im + filt_im * vals_re, tables
    )
    conv = (scale_a * conv_raw + gains * vals_f).astype(BF16)
    corr = inverse(filt_re * dz_re + filt_im * dz_im, filt_re * dz_im - filt_im * dz_re, tables)
    grad_val = (scale_a * corr + gains * dz_f).astype(BF16)
    cross = inverse(vals_re * dz_re + vals_im * dz_im, vals_re * dz_im - vals_im * dz_re, tables)
    return (grad_val, conv, cross)


def per_device_long(values, gates, grad_out, filters, skip):
    length = filters.shape[1]
    scale_a = length ** (-0.5)
    scale_b = (lax.axis_size("dp") * length) ** (-0.5)
    tok_grad = grad_out[0].astype(F32)
    dz_tok = (tok_grad * gates[0].astype(F32)).astype(BF16)
    vals_ch, dz_ch = (
        lax.all_to_all(values[0].T, "ctx", split_axis=0, concat_axis=1, tiled=True),
        lax.all_to_all(dz_tok.T, "ctx", split_axis=0, concat_axis=1, tiled=True),
    )
    grad_val, conv, cross = spectral(
        vals_ch.astype(F32),
        dz_ch.astype(F32),
        filters,
        skip[:, None],
        make_tables(length),
        scale_a,
    )
    total = lax.psum(cross, "dp")
    val_back, conv_back = (
        lax.all_to_all(grad_val, "ctx", split_axis=1, concat_axis=0, tiled=True),
        lax.all_to_all(conv, "ctx", split_axis=1, concat_axis=0, tiled=True),
    )
    grad_gate_tok = (tok_grad * conv_back.T.astype(F32)).astype(BF16)
    return (val_back.T[None], grad_gate_tok[None], scale_b * total)


def dense_tables(half):
    n = np.arange(half, dtype=np.int64)[:, None]
    k = np.concatenate([np.arange(0, half, 2), np.arange(1, half, 2)])[None, :]
    angle = ((2 * k + 1) * n % (4 * half)).astype(np.float64) * (math.pi / (2 * half))
    full = np.concatenate([np.cos(angle), -np.sin(angle)], axis=1).astype(BF16)
    return full, np.ascontiguousarray(full.T)


def vmem_specs(count):
    return [pl.BlockSpec(memory_space=pltpu.VMEM)] * count


def hbm_specs(count):
    return [pl.BlockSpec(memory_space=pl.ANY)] * count


def in_vmem(array):
    return pltpu.with_memory_space_constraint(array, pltpu.VMEM)


def in_hbm(array):
    return pltpu.with_memory_space_constraint(array, pltpu.HBM)


def start_copies(pairs, sems):
    copies = [pltpu.make_async_copy(a, b, sems.at[i]) for i, (a, b) in enumerate(pairs)]
    for copy in copies:
        copy.start()
    return copies


def places(parts):
    me = lax.axis_index("ctx")
    return [
        (f, d, 2 * ((me // 2) ^ d) + ((me % 2) ^ f)) for f in range(2) for d in range(parts // 2)
    ]


def pack_kernel(
    vals_hbm, gate_hbm, grad_hbm, own_ref, sib_ref, grad_ref, vals_ref, gate_ref, turn_ref, sems
):
    pairs, rows, _ = own_ref.shape
    chans = rows // 2
    copies = start_copies(
        [(vals_hbm, vals_ref), (gate_hbm, gate_ref), (grad_hbm, grad_ref)], sems
    )
    copies[0].wait()
    turn_ref[0] = vals_ref[0].astype(F32).T.astype(BF16)
    copies[1].wait()
    copies[2].wait()
    turn_ref[1] = (grad_ref[0].astype(F32) * gate_ref[0].astype(F32)).T.astype(BF16)
    for f, d, at in places(2 * pairs):
        out_ref = sib_ref if f else own_ref
        at = pl.multiple_of(at * chans, chans)
        out_ref[d, :chans, :] = turn_ref[0, pl.ds(at, chans), :]
        out_ref[d, chans:, :] = turn_ref[1, pl.ds(at, chans), :]


def merge_kernel(own_ref, got_ref, *out_refs):
    for d, out_ref in enumerate(out_refs, 1):
        out_ref[0] = own_ref[d]
        out_ref[1] = got_ref[d]


def join_kernel(own_ref, got_ref, out_ref):
    out_ref[:, 0] = own_ref[...]
    out_ref[:, 1] = got_ref[...]


def arrived(own_ref, got_ref, *pair_refs):
    return lambda f, d: pair_refs[-d][f] if d else (got_ref if f else own_ref)[0]


def filter_kernel(
    filt_hbm, fwd_hbm, inv_hbm, skip_ref, spec_ref, fwd_ref, inv_ref, gain_ref, filt_ref, sems
):
    copies = start_copies([(filt_hbm, filt_ref), (fwd_hbm, fwd_ref), (inv_hbm, inv_ref)], sems)
    half = fwd_ref.shape[0]
    copies[0].wait()
    filt = jnp.concatenate([filt_ref[:, :half], filt_ref[:, half:]], axis=0)
    high = filt.astype(BF16)
    low = (filt - high.astype(F32)).astype(BF16)
    copies[1].wait()
    both = jnp.dot(
        jnp.concatenate([high, low], axis=0), fwd_ref[...], preferred_element_type=F32
    )
    spec_ref[...] = both[: filt.shape[0]] + both[filt.shape[0] :]
    chans = filt_ref.shape[0]
    row = lax.broadcasted_iota(jnp.int32, (chans, chans), 0)
    col = lax.broadcasted_iota(jnp.int32, (chans, chans), 1)
    gain = jnp.sum(jnp.where(row == col, skip_ref[...], 0.0), axis=1, keepdims=True)
    gain_ref[...] = jnp.broadcast_to(jnp.concatenate([gain, gain], axis=0), gain_ref.shape)
    copies[2].wait()


def mul(a, b):
    return (a[0] * b[0] - a[1] * b[1], a[0] * b[1] + a[1] * b[0])


def conj_mul(a, b):
    return (a[0] * b[0] + a[1] * b[1], a[0] * b[1] - a[1] * b[0])


def add(a, b):
    return (a[0] + b[0], a[1] + b[1])


def later(a, odd):
    return (a[1], -a[0]) if odd else (-a[1], a[0])


def main_kernel(pairs, *refs):
    fwd_ref, inv_ref, filt_ref, gain_ref = refs[pairs + 1 : pairs + 5]
    own_ref, sib_ref, cross_ref, spec_ref, prod_ref, block_ref = refs[pairs + 5 :]
    parts, rows, pos = block_ref.shape
    chans = rows // 2
    half = parts // 2 * pos
    block = arrived(*refs[: pairs + 1])
    for f, d, at in places(parts):
        block_ref[at] = block(f, d)
    x = [
        jnp.concatenate([block_ref[s] for s in range(parts // 2)], axis=1),
        jnp.concatenate([block_ref[s] for s in range(parts // 2, parts)], axis=1),
    ]
    spec_ref[...] = jnp.dot(
        jnp.concatenate(x, axis=0), fwd_ref[...], preferred_element_type=F32
    )
    inv = inv_ref[...]
    gains = jnp.concatenate([gain_ref[...]] * (half // 128), axis=1)
    scale = (2 * half) ** -0.5 / half

    def products(count, terms):
        for r in range(0, chans, 16):
            for c in range(0, half, 128):

                def load(ref, row):
                    at = slice(row * chans + r, row * chans + r + 16)
                    return (ref[at, c : c + 128], ref[at, half + c : half + c + 128])

                for i, (re, im) in enumerate(terms(load, c >= half // 2)):
                    at = slice(i * chans + r, i * chans + r + 16)
                    prod_ref[at, c : c + 128] = re.astype(BF16)
                    prod_ref[at, half + c : half + c + 128] = im.astype(BF16)
        return jnp.dot(prod_ref[: count * chans], inv, preferred_element_type=F32)

    def with_filter(load, odd):
        v0, g0, v1, g1 = [load(spec_ref, i) for i in range(4)]
        h0, h1 = [load(filt_ref, i) for i in range(2)]
        conv0 = mul(h0, v0)
        conv1 = add(add(mul(h0, v1), mul(h1, v0)), later(conv0, odd))
        corr1 = conj_mul(h0, g1)
        corr0 = add(add(conj_mul(h0, g0), conj_mul(h1, g1)), later(corr1, not odd))
        return (conv0, corr0, conv1, corr1)

    def with_values(load, odd):
        v0, g0, v1, g1 = [load(spec_ref, i) for i in range(4)]
        cross1 = conj_mul(v0, g1)
        cross0 = add(add(conj_mul(v0, g0), conj_mul(v1, g1)), later(cross1, not odd))
        return (cross0, cross1)

    res = products(4, with_filter) * scale
    for i in range(2):
        both = (res[i * rows : (i + 1) * rows] + gains * x[i].astype(F32)).astype(BF16)
        for s in range(parts // 2):
            block_ref[i * (parts // 2) + s] = both[:, s * pos : (s + 1) * pos]
    core = lax.axis_index("ctx") % 2
    for p in range(pairs):
        own_ref[p] = block_ref[2 * p + core]
        sib_ref[p] = block_ref[2 * p + 1 - core]
    res = products(2, with_values) * (1.0 / half)
    for i in range(2):
        cross_ref[:, i * half : (i + 1) * half] = res[i * chans : (i + 1) * chans].astype(BF16)


def pair_kernel(left_ref, right_ref, out_ref):
    out_ref[...] = (left_ref[...].astype(F32) + right_ref[...].astype(F32)).astype(BF16)


def finish_kernel(
    scale,
    left_ref,
    right_ref,
    back_ref,
    near_ref,
    val_hbm,
    gate_hbm,
    filt_hbm,
    val_ref,
    gate_ref,
    filt_ref,
    sems,
):
    pairs, _, rows, _ = back_ref.shape
    chans = rows // 2
    filt_ref[...] = (left_ref[...].astype(F32) + right_ref[...].astype(F32)) * scale
    copies = start_copies([(filt_ref, filt_hbm)], sems)
    core = lax.axis_index("ctx") % 2
    both = [back_ref[p, (core + f) % 2] for p in range(pairs) for f in range(2)]
    vals = jnp.concatenate([block[chans:] for block in both], axis=0)
    val_ref[0] = vals.astype(F32).T.astype(BF16)
    copies += start_copies([(val_ref, val_hbm)], sems.at[pl.ds(1, 1)])
    conv = jnp.concatenate([block[:chans] for block in both], axis=0)
    gate_ref[0] = (near_ref[0].astype(F32) * conv.astype(F32).T).astype(BF16)
    copies += start_copies([(gate_ref, gate_hbm)], sems.at[pl.ds(2, 1)])
    for copy in copies:
        copy.wait()


def call(kernel, name, outs, ins, in_specs, scratch=(), sems=0, flops=0, moved=0):
    return pl.pallas_call(
        kernel,
        out_shape=tuple(
            pltpu.VMEM(shape, dtype) if near else jax.ShapeDtypeStruct(shape, dtype)
            for shape, dtype, near in outs
        ),
        in_specs=in_specs,
        out_specs=tuple(vmem_specs(1)[0] if near else hbm_specs(1)[0] for _, _, near in outs),
        scratch_shapes=[pltpu.VMEM(s, t) for s, t in scratch]
        + ([pltpu.SemaphoreType.DMA((sems,))] if sems else []),
        compiler_params=pltpu.CompilerParams(vmem_limit_bytes=VMEM_BYTES),
        cost_estimate=pl.CostEstimate(flops=flops, bytes_accessed=moved, transcendentals=0),
        name=name,
    )(*ins)


def exchange(own, sib, name):
    pairs, rows, pos = own.shape
    got = lax.ppermute(sib, "ctx", [(j, j ^ 1) for j in range(2 * pairs)])
    sent = call(
        merge_kernel,
        "merge_" + name,
        [((2, rows, pos), BF16, True)] * (pairs - 1),
        (in_vmem(own), in_vmem(got)),
        vmem_specs(2),
        moved=8 * (pairs - 1) * rows * pos,
    )
    held = [
        lax.ppermute(sent[d - 1], "ctx", [(j, j ^ (2 * d)) for j in range(2 * pairs)])
        for d in reversed(range(1, pairs))
    ]
    return [own, got] + held


def dp_pairs(seqs, parts, step):
    pairs = []
    for s in range(seqs):
        for c in range(parts):
            other = s ^ (seqs // 2 // step if c % 2 else step)
            pairs.append((s * parts + c, other * parts + c))
    return pairs


def per_device_short(values, gates, grad_out, filters, skip):
    chans, length = filters.shape
    parts = lax.axis_size("ctx")
    seqs = lax.axis_size("dp")
    _, pos, width = values.shape
    rows = 2 * chans
    fwd, inv = (jnp.asarray(table) for table in dense_tables(length // 2))
    token = ((1, pos, width), BF16)
    pairs = parts // 2
    pair_blocks = ((pairs, rows, pos), BF16)
    turned = ((2, width, pos), BF16)
    own, sib, grad_near = call(
        pack_kernel,
        "pack",
        [(*pair_blocks, True), (*pair_blocks, True), (*token, True)],
        tuple(in_hbm(x) for x in (values, gates, grad_out)),
        hbm_specs(3),
        scratch=[token, token, turned],
        sems=3,
        moved=8 * pos * width,
    )
    held = exchange(own, sib, "out")
    spec, fwd_near, inv_near, gains = call(
        filter_kernel,
        "filter_spectrum",
        [
            ((rows, length), F32, True),
            (fwd.shape, BF16, True),
            (inv.shape, BF16, True),
            ((rows, 128), F32, True),
        ],
        tuple(in_hbm(x) for x in (filters, fwd, inv)) + (skip.reshape(1, chans),),
        hbm_specs(3) + vmem_specs(1),
        scratch=[((chans, length), F32)],
        sems=3,
        flops=4 * chans * length * length,
        moved=8 * length * length,
    )
    own, sib, cross = call(
        functools.partial(main_kernel, pairs),
        "products",
        [(*pair_blocks, True), (*pair_blocks, True), ((chans, length), BF16, True)],
        tuple(in_vmem(x) for x in held + [fwd_near, inv_near, spec, gains]),
        vmem_specs(pairs + 5),
        scratch=[
            ((2 * rows, length), F32),
            ((2 * rows, length), BF16),
            ((parts, rows, pos), BF16),
        ],
        flops=10 * chans * length * length,
        moved=8 * length * length,
    )
    got = lax.ppermute(sib, "ctx", [(j, j ^ 1) for j in range(parts)])
    (sent,) = call(
        join_kernel,
        "join",
        [((pairs, 2, rows, pos), BF16, True)],
        (in_vmem(own), in_vmem(got)),
        vmem_specs(2),
        moved=8 * pairs * rows * pos,
    )
    cores = [list(range(f, parts, 2)) for f in range(2)]
    home = lax.all_to_all(
        sent, "ctx", split_axis=0, concat_axis=0, tiled=True, axis_index_groups=cores
    )
    step = seqs // 2
    while step:
        other = lax.ppermute(cross, ("dp", "ctx"), dp_pairs(seqs, parts, step))
        step //= 2
        if step:
            (cross,) = call(
                pair_kernel,
                "pair_sum",
                [((chans, length), BF16, True)],
                (in_vmem(cross), in_vmem(other)),
                vmem_specs(2),
                moved=6 * chans * length,
            )
    grad_values, grad_gates, grad_filters = call(
        functools.partial(finish_kernel, (seqs * length) ** (-0.5)),
        "finish",
        [(*token, False), (*token, False), ((chans, length), F32, False)],
        tuple(in_vmem(x) for x in (cross, other, home, grad_near)),
        vmem_specs(4),
        scratch=[token, token, ((chans, length), F32)],
        sems=3,
        moved=10 * pos * width + 8 * chans * length,
    )
    return (grad_values, grad_gates, grad_filters)


def per_device(values, gates, grad_out, filters, skip):
    chans, length = filters.shape
    pos = values.shape[1]
    seqs = lax.axis_size("dp")
    dense = length <= DENSE_LIMIT and length % 512 == 0 and chans % 16 == 0 and pos % 128 == 0
    powers = all(n > 1 and n & (n - 1) == 0 for n in (seqs, lax.axis_size("ctx")))
    if dense and powers:
        return per_device_short(values, gates, grad_out, filters, skip)
    return per_device_long(values, gates, grad_out, filters, skip)


def solution(mesh):
    in_specs = (
        P("dp", "ctx", None),
        P("dp", "ctx", None),
        P("dp", "ctx", None),
        P("ctx", None),
        P("ctx"),
    )
    out_specs = (P("dp", "ctx", None), P("dp", "ctx", None), P("ctx", None))
    return jax.shard_map(
        per_device, mesh=mesh, in_specs=in_specs, out_specs=out_specs, check_vma=False
    )
```

```python
import functools
import math

import jax
import jax.numpy as jnp
import numpy as np
from jax import lax
from jax.experimental import pallas as pl
from jax.experimental.pallas import tpu as pltpu
from jax.sharding import PartitionSpec as P

HIGH = lax.Precision.HIGHEST
BF16 = jnp.bfloat16
F32 = jnp.float32
DENSE_LIMIT = 1024
VMEM_BYTES = 16 * 2**20


def twiddle(rows, cols, period):
    left = lax.broadcasted_iota(jnp.int32, (rows, cols), 0)
    right = lax.broadcasted_iota(jnp.int32, (rows, cols), 1)
    angle = (left * right % period).astype(jnp.float32) * (2.0 * math.pi / period)
    return (jnp.cos(angle), jnp.sin(angle))


def pick_first(period):
    best = 2
    for cand in range(2, math.isqrt(period) + 1):
        if period % cand == 0 and cand % 2 == 0:
            best = cand
    return best


def make_tables(length):
    period = 2 * length
    first = pick_first(period)
    second = period // first
    half = first // 2
    return (
        twiddle(half, first, first),
        twiddle(first, second, period),
        twiddle(second, second, second),
        half,
        first,
        second,
        period,
    )


def forward(signal, tables):
    (cos_one, sin_one), (cos_mid, sin_mid), (cos_two, sin_two), half, first, second, period = tables
    shaped = signal.reshape(signal.shape[0], half, second)
    part_re = jnp.einsum("cmn,mk->ckn", shaped, cos_one, precision=HIGH)
    part_im = -jnp.einsum("cmn,mk->ckn", shaped, sin_one, precision=HIGH)
    mid_re = part_re * cos_mid + part_im * sin_mid
    mid_im = part_im * cos_mid - part_re * sin_mid
    spec_re = jnp.einsum("ckn,nm->ckm", mid_re, cos_two, precision=HIGH) + jnp.einsum(
        "ckn,nm->ckm", mid_im, sin_two, precision=HIGH
    )
    spec_im = jnp.einsum("ckn,nm->ckm", mid_im, cos_two, precision=HIGH) - jnp.einsum(
        "ckn,nm->ckm", mid_re, sin_two, precision=HIGH
    )
    return (spec_re, spec_im)


def inverse(spec_re, spec_im, tables):
    (cos_one, sin_one), (cos_mid, sin_mid), (cos_two, sin_two), half, first, second, period = tables
    back_re = jnp.einsum("ckm,nm->ckn", spec_re, cos_two, precision=HIGH) - jnp.einsum(
        "ckm,nm->ckn", spec_im, sin_two, precision=HIGH
    )
    back_im = jnp.einsum("ckm,nm->ckn", spec_im, cos_two, precision=HIGH) + jnp.einsum(
        "ckm,nm->ckn", spec_re, sin_two, precision=HIGH
    )
    turned_re = back_re * cos_mid - back_im * sin_mid
    turned_im = back_im * cos_mid + back_re * sin_mid
    result = jnp.einsum("ckn,mk->cmn", turned_re, cos_one, precision=HIGH) - jnp.einsum(
        "ckn,mk->cmn", turned_im, sin_one, precision=HIGH
    )
    return result.reshape(spec_re.shape[0], half * second) * (1.0 / period)


def spectral(vals_f, dz_f, filt, gains, tables, scale_a):
    vals_re, vals_im = forward(vals_f, tables)
    dz_re, dz_im = forward(dz_f, tables)
    filt_re, filt_im = forward(filt, tables)
    conv_raw = inverse(
        filt_re * vals_re - filt_im * vals_im, filt_re * vals_im + filt_im * vals_re, tables
    )
    conv = (scale_a * conv_raw + gains * vals_f).astype(BF16)
    corr = inverse(filt_re * dz_re + filt_im * dz_im, filt_re * dz_im - filt_im * dz_re, tables)
    grad_val = (scale_a * corr + gains * dz_f).astype(BF16)
    cross = inverse(vals_re * dz_re + vals_im * dz_im, vals_re * dz_im - vals_im * dz_re, tables)
    return (grad_val, conv, cross)


def per_device_long(values, gates, grad_out, filters, skip):
    length = filters.shape[1]
    scale_a = length ** (-0.5)
    scale_b = (lax.axis_size("dp") * length) ** (-0.5)
    tok_grad = grad_out[0].astype(F32)
    dz_tok = (tok_grad * gates[0].astype(F32)).astype(BF16)
    vals_ch, dz_ch = (
        lax.all_to_all(values[0].T, "ctx", split_axis=0, concat_axis=1, tiled=True),
        lax.all_to_all(dz_tok.T, "ctx", split_axis=0, concat_axis=1, tiled=True),
    )
    grad_val, conv, cross = spectral(
        vals_ch.astype(F32),
        dz_ch.astype(F32),
        filters,
        skip[:, None],
        make_tables(length),
        scale_a,
    )
    total = lax.psum(cross, "dp")
    val_back, conv_back = (
        lax.all_to_all(grad_val, "ctx", split_axis=1, concat_axis=0, tiled=True),
        lax.all_to_all(conv, "ctx", split_axis=1, concat_axis=0, tiled=True),
    )
    grad_gate_tok = (tok_grad * conv_back.T.astype(F32)).astype(BF16)
    return (val_back.T[None], grad_gate_tok[None], scale_b * total)


def dense_tables(half):
    n = np.arange(half, dtype=np.int64)[:, None]
    columns = []
    for first in range(2):
        k = np.arange(first, half, 2)[None, :]
        angle = ((2 * k + 1) * n % (4 * half)).astype(np.float64) * (math.pi / (2 * half))
        columns += [np.cos(angle), -np.sin(angle)]
    full = np.concatenate(columns, axis=1).astype(BF16)
    return full, np.ascontiguousarray(full.T)


def vmem_specs(count):
    return [pl.BlockSpec(memory_space=pltpu.VMEM)] * count


def hbm_specs(count):
    return [pl.BlockSpec(memory_space=pl.ANY)] * count


def in_vmem(array):
    return pltpu.with_memory_space_constraint(array, pltpu.VMEM)


def in_hbm(array):
    return pltpu.with_memory_space_constraint(array, pltpu.HBM)


def start_copies(pairs, sems):
    copies = [pltpu.make_async_copy(a, b, sems.at[i]) for i, (a, b) in enumerate(pairs)]
    for copy in copies:
        copy.start()
    return copies


def places(parts):
    me = lax.axis_index("ctx")
    return [
        (f, d, 2 * ((me // 2) ^ d) + ((me % 2) ^ f)) for f in range(2) for d in range(parts // 2)
    ]


def pack_kernel(
    vals_hbm, gate_hbm, grad_hbm, own_ref, sib_ref, grad_ref, vals_ref, gate_ref, turn_ref, sems
):
    pairs, rows, _ = own_ref.shape
    chans = rows // 2
    copies = start_copies(
        [(vals_hbm, vals_ref), (gate_hbm, gate_ref), (grad_hbm, grad_ref)], sems
    )
    copies[0].wait()
    turn_ref[0] = vals_ref[0].astype(F32).T.astype(BF16)
    copies[1].wait()
    copies[2].wait()
    turn_ref[1] = (grad_ref[0].astype(F32) * gate_ref[0].astype(F32)).T.astype(BF16)
    for f, d, at in places(2 * pairs):
        out_ref = sib_ref if f else own_ref
        at = pl.multiple_of(at * chans, chans)
        out_ref[d, :chans, :] = turn_ref[0, pl.ds(at, chans), :]
        out_ref[d, chans:, :] = turn_ref[1, pl.ds(at, chans), :]


def merge_kernel(own_ref, got_ref, *out_refs):
    for d, out_ref in enumerate(out_refs, 1):
        out_ref[0] = own_ref[d]
        out_ref[1] = got_ref[d]


def join_kernel(own_ref, got_ref, out_ref):
    out_ref[:, 0] = own_ref[...]
    out_ref[:, 1] = got_ref[...]


def filter_kernel(
    filt_hbm, fwd_hbm, inv_hbm, skip_ref, spec_ref, fwd_ref, inv_ref, gain_ref, filt_ref, sems
):
    copies = start_copies([(filt_hbm, filt_ref), (fwd_hbm, fwd_ref), (inv_hbm, inv_ref)], sems)
    half = fwd_ref.shape[0]
    copies[0].wait()
    filt = jnp.concatenate([filt_ref[:, :half], filt_ref[:, half:]], axis=0)
    high = filt.astype(BF16)
    low = (filt - high.astype(F32)).astype(BF16)
    copies[1].wait()
    both = jnp.dot(
        jnp.concatenate([high, low], axis=0), fwd_ref[...], preferred_element_type=F32
    )
    spec_ref[...] = both[: filt.shape[0]] + both[filt.shape[0] :]
    chans = filt_ref.shape[0]
    row = lax.broadcasted_iota(jnp.int32, (chans, chans), 0)
    col = lax.broadcasted_iota(jnp.int32, (chans, chans), 1)
    gain = jnp.sum(jnp.where(row == col, skip_ref[...], 0.0), axis=1, keepdims=True)
    gain_ref[...] = jnp.broadcast_to(jnp.concatenate([gain, gain], axis=0), gain_ref.shape)
    copies[2].wait()


def mul(a, b):
    return (a[0] * b[0] - a[1] * b[1], a[0] * b[1] + a[1] * b[0])


def conj_mul(a, b):
    return (a[0] * b[0] + a[1] * b[1], a[0] * b[1] - a[1] * b[0])


def add(a, b):
    return (a[0] + b[0], a[1] + b[1])


def later(a, odd):
    return (a[1], -a[0]) if odd else (-a[1], a[0])


def main_kernel(pairs, *refs):
    fwd_ref, inv_ref, filt_ref, gain_ref = refs[pairs + 1 : pairs + 5]
    own_ref, sib_ref, cross_ref, spec_ref, prod_ref, block_ref = refs[pairs + 5 :]
    parts, rows, pos = block_ref.shape
    chans = rows // 2
    half = parts // 2 * pos
    for f, d, at in places(parts):
        block_ref[at] = refs[pairs + 1 - d][f] if d else refs[f][0]
    x = [
        jnp.concatenate([block_ref[s] for s in range(i, i + parts // 2)], axis=1)
        for i in (0, parts // 2)
    ]
    signals = jnp.concatenate(x, axis=0)
    res = 0.0
    for odd in range(2):
        bins = slice(odd * half, (odd + 1) * half)
        spec_ref[odd] = jnp.dot(signals, fwd_ref[:, bins], preferred_element_type=F32)
        for r in range(0, chans, 16):
            for c in range(0, half // 2, 128):

                def load(ref, row, col):
                    at = slice(row * chans + r, row * chans + r + 16)
                    return [ref[at, i + c : i + c + 128] for i in (col, col + half // 2)]

                v0, g0, v1, g1 = [load(spec_ref.at[odd], i, 0) for i in range(4)]
                h0, h1 = [load(filt_ref, i, odd * half) for i in range(2)]
                conv0 = mul(h0, v0)
                conv1 = add(add(mul(h0, v1), mul(h1, v0)), later(conv0, odd))
                corr1 = conj_mul(h0, g1)
                corr0 = add(add(conj_mul(h0, g0), conj_mul(h1, g1)), later(corr1, not odd))
                cross1 = conj_mul(v0, g1)
                cross0 = add(add(conj_mul(v0, g0), conj_mul(v1, g1)), later(cross1, not odd))
                for i, parts_of in enumerate((conv0, corr0, cross0, conv1, corr1, cross1)):
                    at = slice(i * chans + r, i * chans + r + 16)
                    for col, part in zip((c, c + half // 2), parts_of):
                        prod_ref[odd, at, col : col + 128] = part.astype(BF16)
        res = res + jnp.dot(prod_ref[odd], inv_ref[bins, :], preferred_element_type=F32)
    gains = jnp.concatenate([gain_ref[...]] * (half // 128), axis=1)
    scale = (2 * half) ** -0.5 / half
    for i in range(2):
        top = i * 3 * chans
        both = (res[top : top + rows] * scale + gains * x[i].astype(F32)).astype(BF16)
        for s in range(parts // 2):
            block_ref[i * (parts // 2) + s] = both[:, s * pos : (s + 1) * pos]
        cross = res[top + rows : top + rows + chans] * (1.0 / half)
        cross_ref[:, i * half : (i + 1) * half] = cross.astype(BF16)
    core = lax.axis_index("ctx") % 2
    for p in range(pairs):
        own_ref[p] = block_ref[2 * p + core]
        sib_ref[p] = block_ref[2 * p + 1 - core]


def pair_kernel(left_ref, right_ref, out_ref):
    out_ref[...] = (left_ref[...].astype(F32) + right_ref[...].astype(F32)).astype(BF16)


def finish_kernel(
    scale,
    left_ref,
    right_ref,
    back_ref,
    near_ref,
    val_hbm,
    gate_hbm,
    filt_hbm,
    val_ref,
    gate_ref,
    filt_ref,
    sems,
):
    pairs, _, rows, _ = back_ref.shape
    chans = rows // 2
    filt_ref[...] = (left_ref[...].astype(F32) + right_ref[...].astype(F32)) * scale
    copies = start_copies([(filt_ref, filt_hbm)], sems)
    core = lax.axis_index("ctx") % 2
    both = [back_ref[p, (core + f) % 2] for p in range(pairs) for f in range(2)]
    vals = jnp.concatenate([block[chans:] for block in both], axis=0)
    val_ref[0] = vals.astype(F32).T.astype(BF16)
    copies += start_copies([(val_ref, val_hbm)], sems.at[pl.ds(1, 1)])
    conv = jnp.concatenate([block[:chans] for block in both], axis=0)
    gate_ref[0] = (near_ref[0].astype(F32) * conv.astype(F32).T).astype(BF16)
    copies += start_copies([(gate_ref, gate_hbm)], sems.at[pl.ds(2, 1)])
    for copy in copies:
        copy.wait()


def call(kernel, name, outs, ins, in_specs, scratch=(), sems=0, flops=0, moved=0):
    return pl.pallas_call(
        kernel,
        out_shape=tuple(
            pltpu.VMEM(shape, dtype) if near else jax.ShapeDtypeStruct(shape, dtype)
            for shape, dtype, near in outs
        ),
        in_specs=in_specs,
        out_specs=tuple(vmem_specs(1)[0] if near else hbm_specs(1)[0] for _, _, near in outs),
        scratch_shapes=[pltpu.VMEM(s, t) for s, t in scratch]
        + ([pltpu.SemaphoreType.DMA((sems,))] if sems else []),
        compiler_params=pltpu.CompilerParams(vmem_limit_bytes=VMEM_BYTES),
        cost_estimate=pl.CostEstimate(flops=flops, bytes_accessed=moved, transcendentals=0),
        name=name,
    )(*ins)


def exchange(own, sib, name):
    pairs, rows, pos = own.shape
    got = lax.ppermute(sib, "ctx", [(j, j ^ 1) for j in range(2 * pairs)])
    sent = call(
        merge_kernel,
        "merge_" + name,
        [((2, rows, pos), BF16, True)] * (pairs - 1),
        (in_vmem(own), in_vmem(got)),
        vmem_specs(2),
        moved=8 * (pairs - 1) * rows * pos,
    )
    held = [
        lax.ppermute(sent[d - 1], "ctx", [(j, j ^ (2 * d)) for j in range(2 * pairs)])
        for d in reversed(range(1, pairs))
    ]
    return [own, got] + held


def dp_pairs(seqs, parts, step):
    pairs = []
    for s in range(seqs):
        for c in range(parts):
            other = s ^ (seqs // 2 // step if c % 2 else step)
            pairs.append((s * parts + c, other * parts + c))
    return pairs


def per_device_short(values, gates, grad_out, filters, skip):
    chans, length = filters.shape
    parts = lax.axis_size("ctx")
    seqs = lax.axis_size("dp")
    _, pos, width = values.shape
    rows = 2 * chans
    fwd, inv = (jnp.asarray(table) for table in dense_tables(length // 2))
    token = ((1, pos, width), BF16)
    pairs = parts // 2
    pair_blocks = ((pairs, rows, pos), BF16)
    turned = ((2, width, pos), BF16)
    own, sib, grad_near = call(
        pack_kernel,
        "pack",
        [(*pair_blocks, True), (*pair_blocks, True), (*token, True)],
        tuple(in_hbm(x) for x in (values, gates, grad_out)),
        hbm_specs(3),
        scratch=[token, token, turned],
        sems=3,
        moved=8 * pos * width,
    )
    held = exchange(own, sib, "out")
    spec, fwd_near, inv_near, gains = call(
        filter_kernel,
        "filter_spectrum",
        [
            ((rows, length), F32, True),
            (fwd.shape, BF16, True),
            (inv.shape, BF16, True),
            ((rows, 128), F32, True),
        ],
        tuple(in_hbm(x) for x in (filters, fwd, inv)) + (skip.reshape(1, chans),),
        hbm_specs(3) + vmem_specs(1),
        scratch=[((chans, length), F32)],
        sems=3,
        flops=4 * chans * length * length,
        moved=8 * length * length,
    )
    own, sib, cross = call(
        functools.partial(main_kernel, pairs),
        "products",
        [(*pair_blocks, True), (*pair_blocks, True), ((chans, length), BF16, True)],
        tuple(in_vmem(x) for x in held + [fwd_near, inv_near, spec, gains]),
        vmem_specs(pairs + 5),
        scratch=[
            ((2, 2 * rows, length // 2), F32),
            ((2, 3 * rows, length // 2), BF16),
            ((parts, rows, pos), BF16),
        ],
        flops=10 * chans * length * length,
        moved=8 * length * length,
    )
    got = lax.ppermute(sib, "ctx", [(j, j ^ 1) for j in range(parts)])
    (sent,) = call(
        join_kernel,
        "join",
        [((pairs, 2, rows, pos), BF16, True)],
        (in_vmem(own), in_vmem(got)),
        vmem_specs(2),
        moved=8 * pairs * rows * pos,
    )
    cores = [list(range(f, parts, 2)) for f in range(2)]
    home = lax.all_to_all(
        sent, "ctx", split_axis=0, concat_axis=0, tiled=True, axis_index_groups=cores
    )
    step = seqs // 2
    while step:
        other = lax.ppermute(cross, ("dp", "ctx"), dp_pairs(seqs, parts, step))
        step //= 2
        if step:
            (cross,) = call(
                pair_kernel,
                "pair_sum",
                [((chans, length), BF16, True)],
                (in_vmem(cross), in_vmem(other)),
                vmem_specs(2),
                moved=6 * chans * length,
            )
    grad_values, grad_gates, grad_filters = call(
        functools.partial(finish_kernel, (seqs * length) ** (-0.5)),
        "finish",
        [(*token, False), (*token, False), ((chans, length), F32, False)],
        tuple(in_vmem(x) for x in (cross, other, home, grad_near)),
        vmem_specs(4),
        scratch=[token, token, ((chans, length), F32)],
        sems=3,
        moved=10 * pos * width + 8 * chans * length,
    )
    return (grad_values, grad_gates, grad_filters)


def per_device(values, gates, grad_out, filters, skip):
    chans, length = filters.shape
    pos = values.shape[1]
    seqs = lax.axis_size("dp")
    dense = length <= DENSE_LIMIT and length % 512 == 0 and chans % 16 == 0 and pos % 128 == 0
    powers = all(n > 1 and n & (n - 1) == 0 for n in (seqs, lax.axis_size("ctx")))
    if dense and powers:
        return per_device_short(values, gates, grad_out, filters, skip)
    return per_device_long(values, gates, grad_out, filters, skip)


def solution(mesh):
    in_specs = (
        P("dp", "ctx", None),
        P("dp", "ctx", None),
        P("dp", "ctx", None),
        P("ctx", None),
        P("ctx"),
    )
    out_specs = (P("dp", "ctx", None), P("dp", "ctx", None), P("ctx", None))
    return jax.shard_map(
        per_device, mesh=mesh, in_specs=in_specs, out_specs=out_specs, check_vma=False
    )
```

```python
import functools
import math

import jax
import jax.numpy as jnp
import numpy as np
from jax import lax
from jax.experimental import pallas as pl
from jax.experimental.pallas import tpu as pltpu
from jax.sharding import PartitionSpec as P

HIGH = lax.Precision.HIGHEST
BF16 = jnp.bfloat16
F32 = jnp.float32
DENSE_LIMIT = 1024
VMEM_BYTES = 16 * 2**20
UNPACK_COST = 5 * 10**9


def twiddle(rows, cols, period):
    left = lax.broadcasted_iota(jnp.int32, (rows, cols), 0)
    right = lax.broadcasted_iota(jnp.int32, (rows, cols), 1)
    angle = (left * right % period).astype(jnp.float32) * (2.0 * math.pi / period)
    return (jnp.cos(angle), jnp.sin(angle))


def pick_first(period):
    best = 2
    for cand in range(2, math.isqrt(period) + 1):
        if period % cand == 0 and cand % 2 == 0:
            best = cand
    return best


def make_tables(length):
    period = 2 * length
    first = pick_first(period)
    second = period // first
    half = first // 2
    return (
        twiddle(half, first, first),
        twiddle(first, second, period),
        twiddle(second, second, second),
        half,
        first,
        second,
        period,
    )


def forward(signal, tables):
    (cos_one, sin_one), (cos_mid, sin_mid), (cos_two, sin_two), half, first, second, period = tables
    shaped = signal.reshape(signal.shape[0], half, second)
    part_re = jnp.einsum("cmn,mk->ckn", shaped, cos_one, precision=HIGH)
    part_im = -jnp.einsum("cmn,mk->ckn", shaped, sin_one, precision=HIGH)
    mid_re = part_re * cos_mid + part_im * sin_mid
    mid_im = part_im * cos_mid - part_re * sin_mid
    spec_re = jnp.einsum("ckn,nm->ckm", mid_re, cos_two, precision=HIGH) + jnp.einsum(
        "ckn,nm->ckm", mid_im, sin_two, precision=HIGH
    )
    spec_im = jnp.einsum("ckn,nm->ckm", mid_im, cos_two, precision=HIGH) - jnp.einsum(
        "ckn,nm->ckm", mid_re, sin_two, precision=HIGH
    )
    return (spec_re, spec_im)


def inverse(spec_re, spec_im, tables):
    (cos_one, sin_one), (cos_mid, sin_mid), (cos_two, sin_two), half, first, second, period = tables
    back_re = jnp.einsum("ckm,nm->ckn", spec_re, cos_two, precision=HIGH) - jnp.einsum(
        "ckm,nm->ckn", spec_im, sin_two, precision=HIGH
    )
    back_im = jnp.einsum("ckm,nm->ckn", spec_im, cos_two, precision=HIGH) + jnp.einsum(
        "ckm,nm->ckn", spec_re, sin_two, precision=HIGH
    )
    turned_re = back_re * cos_mid - back_im * sin_mid
    turned_im = back_im * cos_mid + back_re * sin_mid
    result = jnp.einsum("ckn,mk->cmn", turned_re, cos_one, precision=HIGH) - jnp.einsum(
        "ckn,mk->cmn", turned_im, sin_one, precision=HIGH
    )
    return result.reshape(spec_re.shape[0], half * second) * (1.0 / period)


def spectral(vals_f, dz_f, filt, gains, tables, scale_a):
    vals_re, vals_im = forward(vals_f, tables)
    dz_re, dz_im = forward(dz_f, tables)
    filt_re, filt_im = forward(filt, tables)
    conv_raw = inverse(
        filt_re * vals_re - filt_im * vals_im, filt_re * vals_im + filt_im * vals_re, tables
    )
    conv = (scale_a * conv_raw + gains * vals_f).astype(BF16)
    corr = inverse(filt_re * dz_re + filt_im * dz_im, filt_re * dz_im - filt_im * dz_re, tables)
    grad_val = (scale_a * corr + gains * dz_f).astype(BF16)
    cross = inverse(vals_re * dz_re + vals_im * dz_im, vals_re * dz_im - vals_im * dz_re, tables)
    return (grad_val, conv, cross)


def per_device_long(values, gates, grad_out, filters, skip):
    length = filters.shape[1]
    scale_a = length ** (-0.5)
    scale_b = (lax.axis_size("dp") * length) ** (-0.5)
    tok_grad = grad_out[0].astype(F32)
    dz_tok = (tok_grad * gates[0].astype(F32)).astype(BF16)
    vals_ch, dz_ch = (
        lax.all_to_all(values[0].T, "ctx", split_axis=0, concat_axis=1, tiled=True),
        lax.all_to_all(dz_tok.T, "ctx", split_axis=0, concat_axis=1, tiled=True),
    )
    grad_val, conv, cross = spectral(
        vals_ch.astype(F32),
        dz_ch.astype(F32),
        filters,
        skip[:, None],
        make_tables(length),
        scale_a,
    )
    total = lax.psum(cross, "dp")
    val_back, conv_back = (
        lax.all_to_all(grad_val, "ctx", split_axis=1, concat_axis=0, tiled=True),
        lax.all_to_all(conv, "ctx", split_axis=1, concat_axis=0, tiled=True),
    )
    grad_gate_tok = (tok_grad * conv_back.T.astype(F32)).astype(BF16)
    return (val_back.T[None], grad_gate_tok[None], scale_b * total)


def dense_tables(half):
    n = np.arange(half, dtype=np.int64)[:, None]
    columns = []
    for first in range(2):
        k = np.arange(first, half, 2)[None, :]
        angle = ((2 * k + 1) * n % (4 * half)).astype(np.float64) * (math.pi / (2 * half))
        columns += [np.cos(angle), -np.sin(angle)]
    full = np.concatenate(columns, axis=1).astype(BF16)
    return full, np.ascontiguousarray(full.T)


def vmem_specs(count):
    return [pl.BlockSpec(memory_space=pltpu.VMEM)] * count


def hbm_specs(count):
    return [pl.BlockSpec(memory_space=pl.ANY)] * count


def in_vmem(array):
    return pltpu.with_memory_space_constraint(array, pltpu.VMEM)


def in_hbm(array):
    return pltpu.with_memory_space_constraint(array, pltpu.HBM)


def start_copies(pairs, sems):
    copies = [pltpu.make_async_copy(a, b, sems.at[i]) for i, (a, b) in enumerate(pairs)]
    for copy in copies:
        copy.start()
    return copies


def places(parts):
    me = lax.axis_index("ctx")
    return [
        (f, d, 2 * ((me // 2) ^ d) + ((me % 2) ^ f)) for f in range(2) for d in range(parts // 2)
    ]


def pack_kernel(
    vals_hbm, gate_hbm, grad_hbm, own_ref, sib_ref, grad_ref, vals_ref, gate_ref, turn_ref, sems
):
    pairs, rows, _ = own_ref.shape
    chans = rows // 2
    copies = start_copies(
        [(vals_hbm, vals_ref), (gate_hbm, gate_ref), (grad_hbm, grad_ref)], sems
    )
    copies[0].wait()
    turn_ref[0] = vals_ref[0].astype(F32).T.astype(BF16)
    copies[1].wait()
    copies[2].wait()
    turn_ref[1] = (grad_ref[0].astype(F32) * gate_ref[0].astype(F32)).T.astype(BF16)
    for f, d, at in places(2 * pairs):
        out_ref = sib_ref if f else own_ref
        at = pl.multiple_of(at * chans, chans)
        out_ref[d, :chans, :] = turn_ref[0, pl.ds(at, chans), :]
        out_ref[d, chans:, :] = turn_ref[1, pl.ds(at, chans), :]


def merge_kernel(own_ref, got_ref, *out_refs):
    for d, out_ref in enumerate(out_refs, 1):
        out_ref[0] = own_ref[d]
        out_ref[1] = got_ref[d]


def filter_kernel(
    filt_hbm, fwd_hbm, inv_hbm, skip_ref, spec_ref, fwd_ref, inv_ref, gain_ref, filt_ref, sems
):
    copies = start_copies([(filt_hbm, filt_ref), (fwd_hbm, fwd_ref), (inv_hbm, inv_ref)], sems)
    half = fwd_ref.shape[0]
    copies[0].wait()
    filt = jnp.concatenate([filt_ref[:, :half], filt_ref[:, half:]], axis=0)
    high = filt.astype(BF16)
    low = (filt - high.astype(F32)).astype(BF16)
    copies[1].wait()
    both = jnp.dot(
        jnp.concatenate([high, low], axis=0), fwd_ref[...], preferred_element_type=F32
    )
    spec_ref[...] = both[: filt.shape[0]] + both[filt.shape[0] :]
    chans = filt_ref.shape[0]
    row = lax.broadcasted_iota(jnp.int32, (chans, chans), 0)
    col = lax.broadcasted_iota(jnp.int32, (chans, chans), 1)
    gain = jnp.sum(jnp.where(row == col, skip_ref[...], 0.0), axis=1, keepdims=True)
    gain_ref[...] = jnp.broadcast_to(jnp.concatenate([gain, gain], axis=0), gain_ref.shape)
    copies[2].wait()


def mul(a, b):
    return (a[0] * b[0] - a[1] * b[1], a[0] * b[1] + a[1] * b[0])


def conj_mul(a, b):
    return (a[0] * b[0] + a[1] * b[1], a[0] * b[1] - a[1] * b[0])


def add(a, b):
    return (a[0] + b[0], a[1] + b[1])


def later(a, odd):
    return (a[1], -a[0]) if odd else (-a[1], a[0])


def main_kernel(pairs, *refs):
    fwd_ref, inv_ref, filt_ref, gain_ref = refs[pairs + 1 : pairs + 5]
    own_ref, sib_ref, cross_ref, spec_ref, prod_ref, block_ref = refs[pairs + 5 :]
    parts, rows, pos = block_ref.shape
    chans = rows // 2
    half = parts // 2 * pos
    for f, d, at in places(parts):
        block_ref[at] = refs[pairs + 1 - d][f] if d else refs[f][0]
    x = [
        jnp.concatenate([block_ref[s] for s in range(i, i + parts // 2)], axis=1)
        for i in (0, parts // 2)
    ]
    signals = jnp.concatenate(x, axis=0)
    res = 0.0
    for odd in range(2):
        bins = slice(odd * half, (odd + 1) * half)
        spec_ref[odd] = jnp.dot(signals, fwd_ref[:, bins], preferred_element_type=F32)
        for r in range(0, chans, 16):
            for c in range(0, half // 2, 128):

                def load(ref, row, col):
                    at = slice(row * chans + r, row * chans + r + 16)
                    return [ref[at, i + c : i + c + 128] for i in (col, col + half // 2)]

                v0, g0, v1, g1 = [load(spec_ref.at[odd], i, 0) for i in range(4)]
                h0, h1 = [load(filt_ref, i, odd * half) for i in range(2)]
                conv0 = mul(h0, v0)
                conv1 = add(add(mul(h0, v1), mul(h1, v0)), later(conv0, odd))
                corr1 = conj_mul(h0, g1)
                corr0 = add(add(conj_mul(h0, g0), conj_mul(h1, g1)), later(corr1, not odd))
                cross1 = conj_mul(v0, g1)
                cross0 = add(add(conj_mul(v0, g0), conj_mul(v1, g1)), later(cross1, not odd))
                for i, parts_of in enumerate((conv0, corr0, cross0, conv1, corr1, cross1)):
                    at = slice(i * chans + r, i * chans + r + 16)
                    for col, part in zip((c, c + half // 2), parts_of):
                        prod_ref[odd, at, col : col + 128] = part.astype(BF16)
        res = res + jnp.dot(prod_ref[odd], inv_ref[bins, :], preferred_element_type=F32)
    gains = jnp.concatenate([gain_ref[...]] * (half // 128), axis=1)
    scale = (2 * half) ** -0.5 / half
    for i in range(2):
        top = i * 3 * chans
        both = (res[top : top + rows] * scale + gains * x[i].astype(F32)).astype(BF16)
        for s in range(parts // 2):
            block_ref[i * (parts // 2) + s] = both[:, s * pos : (s + 1) * pos]
        cross = res[top + rows : top + rows + chans] * (1.0 / half)
        cross_ref[:, i * half : (i + 1) * half] = cross.astype(BF16)
    for f, d, at in places(parts):
        (sib_ref if f else own_ref)[d] = block_ref[at]


def pair_kernel(left_ref, right_ref, out_ref):
    out_ref[...] = (left_ref[...].astype(F32) + right_ref[...].astype(F32)).astype(BF16)


def unpack_kernel(pairs, *refs):
    near_ref, val_hbm, gate_hbm, val_ref, gate_ref, turn_ref, sems = refs[pairs + 1 :]
    chans = turn_ref.shape[1] // (2 * pairs)
    for f, d, at in places(2 * pairs):
        at = pl.multiple_of(at * chans, chans)
        both = refs[pairs + 1 - d][f] if d else refs[f][0]
        turn_ref[0, pl.ds(at, chans), :] = both[:chans]
        turn_ref[1, pl.ds(at, chans), :] = both[chans:]
    val_ref[0] = turn_ref[1].astype(F32).T.astype(BF16)
    copies = start_copies([(val_ref, val_hbm)], sems)
    gate_ref[0] = (near_ref[0].astype(F32) * turn_ref[0].astype(F32).T).astype(BF16)
    copies += start_copies([(gate_ref, gate_hbm)], sems.at[pl.ds(1, 1)])
    for copy in copies:
        copy.wait()


def total_kernel(scale, left_ref, right_ref, _, out_hbm, out_ref, sems):
    cuts = sems.shape[0]
    each = out_ref.shape[0] // cuts
    copies = []
    for i in range(cuts):
        at = pl.ds(i * each, each)
        out_ref[at, :] = (left_ref[at, :].astype(F32) + right_ref[at, :].astype(F32)) * scale
        copies += start_copies([(out_ref.at[at, :], out_hbm.at[at, :])], sems.at[pl.ds(i, 1)])
    for copy in copies:
        copy.wait()


def call(kernel, name, outs, ins, in_specs, scratch=(), sems=0, flops=0, moved=0):
    return pl.pallas_call(
        kernel,
        out_shape=tuple(
            pltpu.VMEM(shape, dtype) if near else jax.ShapeDtypeStruct(shape, dtype)
            for shape, dtype, near in outs
        ),
        in_specs=in_specs,
        out_specs=tuple(vmem_specs(1)[0] if near else hbm_specs(1)[0] for _, _, near in outs),
        scratch_shapes=[pltpu.VMEM(s, t) for s, t in scratch]
        + ([pltpu.SemaphoreType.DMA((sems,))] if sems else []),
        compiler_params=pltpu.CompilerParams(vmem_limit_bytes=VMEM_BYTES),
        cost_estimate=pl.CostEstimate(flops=flops, bytes_accessed=moved, transcendentals=0),
        name=name,
    )(*ins)


def exchange(own, sib, name):
    pairs, rows, pos = own.shape
    got = lax.ppermute(sib, "ctx", [(j, j ^ 1) for j in range(2 * pairs)])
    sent = call(
        merge_kernel,
        "merge_" + name,
        [((2, rows, pos), BF16, True)] * (pairs - 1),
        (in_vmem(own), in_vmem(got)),
        vmem_specs(2),
        moved=8 * (pairs - 1) * rows * pos,
    )
    held = [
        lax.ppermute(sent[d - 1], "ctx", [(j, j ^ (2 * d)) for j in range(2 * pairs)])
        for d in reversed(range(1, pairs))
    ]
    return [own, got] + held


def dp_pairs(seqs, parts, step):
    masks = (step, 2 * (seqs // 2 // step) - 1)
    return [
        (s * parts + c, (s ^ masks[c % 2]) * parts + c) for s in range(seqs) for c in range(parts)
    ]


def per_device_short(values, gates, grad_out, filters, skip):
    chans, length = filters.shape
    parts = lax.axis_size("ctx")
    seqs = lax.axis_size("dp")
    _, pos, width = values.shape
    rows = 2 * chans
    fwd, inv = (jnp.asarray(table) for table in dense_tables(length // 2))
    token = ((1, pos, width), BF16)
    pairs = parts // 2
    pair_blocks = ((pairs, rows, pos), BF16)
    turned = ((2, width, pos), BF16)
    own, sib, grad_near = call(
        pack_kernel,
        "pack",
        [(*pair_blocks, True), (*pair_blocks, True), (*token, True)],
        tuple(in_hbm(x) for x in (values, gates, grad_out)),
        hbm_specs(3),
        scratch=[token, token, turned],
        sems=3,
        moved=8 * pos * width,
    )
    held = exchange(own, sib, "out")
    spec, fwd_near, inv_near, gains = call(
        filter_kernel,
        "filter_spectrum",
        [
            ((rows, length), F32, True),
            (fwd.shape, BF16, True),
            (inv.shape, BF16, True),
            ((rows, 128), F32, True),
        ],
        tuple(in_hbm(x) for x in (filters, fwd, inv)) + (skip.reshape(1, chans),),
        hbm_specs(3) + vmem_specs(1),
        scratch=[((chans, length), F32)],
        sems=3,
        flops=4 * chans * length * length,
        moved=8 * length * length,
    )
    own, sib, cross = call(
        functools.partial(main_kernel, pairs),
        "products",
        [(*pair_blocks, True), (*pair_blocks, True), ((chans, length), BF16, True)],
        tuple(in_vmem(x) for x in held + [fwd_near, inv_near, spec, gains]),
        vmem_specs(pairs + 5),
        scratch=[
            ((2, 2 * rows, length // 2), F32),
            ((2, 3 * rows, length // 2), BF16),
            ((parts, rows, pos), BF16),
        ],
        flops=10 * chans * length * length,
        moved=8 * length * length,
    )
    home = exchange(own, sib, "home")
    step = seqs // 2
    while step:
        other = lax.ppermute(cross, ("dp", "ctx"), dp_pairs(seqs, parts, step))
        step //= 2
        if step:
            (cross,) = call(
                pair_kernel,
                "pair_sum",
                [((chans, length), BF16, True)],
                (in_vmem(cross), in_vmem(other)),
                vmem_specs(2),
                moved=6 * chans * length,
            )
    grad_values, grad_gates = call(
        functools.partial(unpack_kernel, pairs),
        "unpack",
        [(*token, False), (*token, False)],
        tuple(in_vmem(x) for x in home + [grad_near]),
        vmem_specs(pairs + 2),
        scratch=[token, token, turned],
        sems=2,
        flops=UNPACK_COST,
        moved=10 * pos * width,
    )
    (grad_filters,) = call(
        functools.partial(total_kernel, (seqs * length) ** (-0.5)),
        "total",
        [((chans, length), F32, False)],
        (in_vmem(cross), in_vmem(other), in_hbm(grad_gates)),
        vmem_specs(2) + hbm_specs(1),
        scratch=[((chans, length), F32)],
        sems=4,
        moved=8 * chans * length,
    )
    return (grad_values, grad_gates, grad_filters)


def per_device(values, gates, grad_out, filters, skip):
    chans, length = filters.shape
    pos = values.shape[1]
    seqs = lax.axis_size("dp")
    dense = length <= DENSE_LIMIT and length % 512 == 0 and chans % 16 == 0 and pos % 128 == 0
    powers = all(n > 1 and n & (n - 1) == 0 for n in (seqs, lax.axis_size("ctx")))
    if dense and powers:
        return per_device_short(values, gates, grad_out, filters, skip)
    return per_device_long(values, gates, grad_out, filters, skip)


def solution(mesh):
    in_specs = (
        P("dp", "ctx", None),
        P("dp", "ctx", None),
        P("dp", "ctx", None),
        P("ctx", None),
        P("ctx"),
    )
    out_specs = (P("dp", "ctx", None), P("dp", "ctx", None), P("ctx", None))
    return jax.shard_map(
        per_device, mesh=mesh, in_specs=in_specs, out_specs=out_specs, check_vma=False
    )
```

```python
import functools
import math

import jax
import jax.numpy as jnp
import numpy as np
from jax import lax
from jax.experimental import pallas as pl
from jax.experimental.pallas import tpu as pltpu
from jax.sharding import PartitionSpec as P

HIGH = lax.Precision.HIGHEST
BF16 = jnp.bfloat16
F32 = jnp.float32
DENSE_LIMIT = 1024
VMEM_BYTES = 16 * 2**20
UNPACK_COST = 5 * 10**9


def twiddle(rows, cols, period):
    left = lax.broadcasted_iota(jnp.int32, (rows, cols), 0)
    right = lax.broadcasted_iota(jnp.int32, (rows, cols), 1)
    angle = (left * right % period).astype(jnp.float32) * (2.0 * math.pi / period)
    return (jnp.cos(angle), jnp.sin(angle))


def pick_first(period):
    best = 2
    for cand in range(2, math.isqrt(period) + 1):
        if period % cand == 0 and cand % 2 == 0:
            best = cand
    return best


def make_tables(length):
    period = 2 * length
    first = pick_first(period)
    second = period // first
    half = first // 2
    return (
        twiddle(half, first, first),
        twiddle(first, second, period),
        twiddle(second, second, second),
        half,
        first,
        second,
        period,
    )


def forward(signal, tables):
    (cos_one, sin_one), (cos_mid, sin_mid), (cos_two, sin_two), half, first, second, period = tables
    shaped = signal.reshape(signal.shape[0], half, second)
    part_re = jnp.einsum("cmn,mk->ckn", shaped, cos_one, precision=HIGH)
    part_im = -jnp.einsum("cmn,mk->ckn", shaped, sin_one, precision=HIGH)
    mid_re = part_re * cos_mid + part_im * sin_mid
    mid_im = part_im * cos_mid - part_re * sin_mid
    spec_re = jnp.einsum("ckn,nm->ckm", mid_re, cos_two, precision=HIGH) + jnp.einsum(
        "ckn,nm->ckm", mid_im, sin_two, precision=HIGH
    )
    spec_im = jnp.einsum("ckn,nm->ckm", mid_im, cos_two, precision=HIGH) - jnp.einsum(
        "ckn,nm->ckm", mid_re, sin_two, precision=HIGH
    )
    return (spec_re, spec_im)


def inverse(spec_re, spec_im, tables):
    (cos_one, sin_one), (cos_mid, sin_mid), (cos_two, sin_two), half, first, second, period = tables
    back_re = jnp.einsum("ckm,nm->ckn", spec_re, cos_two, precision=HIGH) - jnp.einsum(
        "ckm,nm->ckn", spec_im, sin_two, precision=HIGH
    )
    back_im = jnp.einsum("ckm,nm->ckn", spec_im, cos_two, precision=HIGH) + jnp.einsum(
        "ckm,nm->ckn", spec_re, sin_two, precision=HIGH
    )
    turned_re = back_re * cos_mid - back_im * sin_mid
    turned_im = back_im * cos_mid + back_re * sin_mid
    result = jnp.einsum("ckn,mk->cmn", turned_re, cos_one, precision=HIGH) - jnp.einsum(
        "ckn,mk->cmn", turned_im, sin_one, precision=HIGH
    )
    return result.reshape(spec_re.shape[0], half * second) * (1.0 / period)


def spectral(vals_f, dz_f, filt, gains, tables, scale_a):
    vals_re, vals_im = forward(vals_f, tables)
    dz_re, dz_im = forward(dz_f, tables)
    filt_re, filt_im = forward(filt, tables)
    conv_raw = inverse(
        filt_re * vals_re - filt_im * vals_im, filt_re * vals_im + filt_im * vals_re, tables
    )
    conv = (scale_a * conv_raw + gains * vals_f).astype(BF16)
    corr = inverse(filt_re * dz_re + filt_im * dz_im, filt_re * dz_im - filt_im * dz_re, tables)
    grad_val = (scale_a * corr + gains * dz_f).astype(BF16)
    cross = inverse(vals_re * dz_re + vals_im * dz_im, vals_re * dz_im - vals_im * dz_re, tables)
    return (grad_val, conv, cross)


def per_device_long(values, gates, grad_out, filters, skip):
    length = filters.shape[1]
    scale_a = length ** (-0.5)
    scale_b = (lax.axis_size("dp") * length) ** (-0.5)
    tok_grad = grad_out[0].astype(F32)
    dz_tok = (tok_grad * gates[0].astype(F32)).astype(BF16)
    vals_ch, dz_ch = (
        lax.all_to_all(values[0].T, "ctx", split_axis=0, concat_axis=1, tiled=True),
        lax.all_to_all(dz_tok.T, "ctx", split_axis=0, concat_axis=1, tiled=True),
    )
    grad_val, conv, cross = spectral(
        vals_ch.astype(F32),
        dz_ch.astype(F32),
        filters,
        skip[:, None],
        make_tables(length),
        scale_a,
    )
    total = lax.psum(cross, "dp")
    val_back, conv_back = (
        lax.all_to_all(grad_val, "ctx", split_axis=1, concat_axis=0, tiled=True),
        lax.all_to_all(conv, "ctx", split_axis=1, concat_axis=0, tiled=True),
    )
    grad_gate_tok = (tok_grad * conv_back.T.astype(F32)).astype(BF16)
    return (val_back.T[None], grad_gate_tok[None], scale_b * total)


def dense_tables(half):
    n = np.arange(half, dtype=np.int64)[:, None]
    columns = []
    for first in range(2):
        k = np.arange(first, half, 2)[None, :]
        angle = ((2 * k + 1) * n % (4 * half)).astype(np.float64) * (math.pi / (2 * half))
        columns += [np.cos(angle), -np.sin(angle)]
    full = np.concatenate(columns, axis=1).astype(BF16)
    return full, np.ascontiguousarray(full.T)


def vmem_specs(count):
    return [pl.BlockSpec(memory_space=pltpu.VMEM)] * count


def hbm_specs(count):
    return [pl.BlockSpec(memory_space=pl.ANY)] * count


def in_vmem(array):
    return pltpu.with_memory_space_constraint(array, pltpu.VMEM)


def in_hbm(array):
    return pltpu.with_memory_space_constraint(array, pltpu.HBM)


def start_copies(pairs, sems):
    copies = [pltpu.make_async_copy(a, b, sems.at[i]) for i, (a, b) in enumerate(pairs)]
    for copy in copies:
        copy.start()
    return copies


def places(parts):
    me = lax.axis_index("ctx")
    return [
        (f, d, 2 * ((me // 2) ^ d) + ((me % 2) ^ f)) for f in range(2) for d in range(parts // 2)
    ]


def pack_kernel(
    vals_hbm, gate_hbm, grad_hbm, own_ref, sib_ref, grad_ref, vals_ref, gate_ref, turn_ref, sems
):
    pairs, rows, _ = own_ref.shape
    chans = rows // 2
    copies = start_copies(
        [(vals_hbm, vals_ref), (gate_hbm, gate_ref), (grad_hbm, grad_ref)], sems
    )
    copies[0].wait()
    turn_ref[0] = vals_ref[0].astype(F32).T.astype(BF16)
    copies[1].wait()
    copies[2].wait()
    turn_ref[1] = (grad_ref[0].astype(F32) * gate_ref[0].astype(F32)).T.astype(BF16)
    for f, d, at in places(2 * pairs):
        out_ref = sib_ref if f else own_ref
        at = pl.multiple_of(at * chans, chans)
        out_ref[d, :chans, :] = turn_ref[0, pl.ds(at, chans), :]
        out_ref[d, chans:, :] = turn_ref[1, pl.ds(at, chans), :]


def merge_kernel(own_ref, got_ref, *out_refs):
    for d, out_ref in enumerate(out_refs, 1):
        out_ref[0] = own_ref[d]
        out_ref[1] = got_ref[d]


def filter_kernel(
    filt_hbm, fwd_hbm, inv_hbm, skip_ref, spec_ref, fwd_ref, inv_ref, gain_ref, filt_ref, sems
):
    copies = start_copies([(filt_hbm, filt_ref), (fwd_hbm, fwd_ref), (inv_hbm, inv_ref)], sems)
    half = fwd_ref.shape[0]
    copies[0].wait()
    filt = jnp.concatenate([filt_ref[:, :half], filt_ref[:, half:]], axis=0)
    high = filt.astype(BF16)
    low = (filt - high.astype(F32)).astype(BF16)
    copies[1].wait()
    both = jnp.dot(
        jnp.concatenate([high, low], axis=0), fwd_ref[...], preferred_element_type=F32
    )
    spec_ref[...] = both[: filt.shape[0]] + both[filt.shape[0] :]
    chans = filt_ref.shape[0]
    row = lax.broadcasted_iota(jnp.int32, (chans, chans), 0)
    col = lax.broadcasted_iota(jnp.int32, (chans, chans), 1)
    gain = jnp.sum(jnp.where(row == col, skip_ref[...], 0.0), axis=1, keepdims=True)
    gain_ref[...] = jnp.broadcast_to(jnp.concatenate([gain, gain], axis=0), gain_ref.shape)
    copies[2].wait()


def mul(a, b):
    return (a[0] * b[0] - a[1] * b[1], a[0] * b[1] + a[1] * b[0])


def conj_mul(a, b):
    return (a[0] * b[0] + a[1] * b[1], a[0] * b[1] - a[1] * b[0])


def add(a, b):
    return (a[0] + b[0], a[1] + b[1])


def later(a, odd):
    return (a[1], -a[0]) if odd else (-a[1], a[0])


def main_kernel(pairs, home, *refs):
    fwd_ref, inv_ref = refs[pairs + 1 : pairs + 3]
    if home:
        filt_ref, gain_ref, _, own_ref, sib_ref, *sent_refs = refs[pairs + 3 : -3]
    else:
        (cross_ref,) = refs[pairs + 3 : -3]
    spec_ref, prod_ref, block_ref = refs[-3:]
    parts, rows, pos = block_ref.shape
    chans = rows // 2
    half = parts // 2 * pos
    for f, d, at in places(parts):
        block_ref[at] = refs[pairs + 1 - d][f] if d else refs[f][0]
    x = [
        jnp.concatenate([block_ref[s] for s in range(i, i + parts // 2)], axis=1)
        for i in (0, parts // 2)
    ]
    signals = jnp.concatenate(x, axis=0)
    res = 0.0
    for odd in range(2):
        bins = slice(odd * half, (odd + 1) * half)
        spec_ref[odd] = jnp.dot(signals, fwd_ref[:, bins], preferred_element_type=F32)
        for r in range(0, chans, 16):
            for c in range(0, half // 2, 128):

                def load(ref, row, col):
                    at = slice(row * chans + r, row * chans + r + 16)
                    return [ref[at, i + c : i + c + 128] for i in (col, col + half // 2)]

                v0, g0, v1, g1 = [load(spec_ref.at[odd], i, 0) for i in range(4)]
                if home:
                    h0, h1 = [load(filt_ref, i, odd * half) for i in range(2)]
                    conv0 = mul(h0, v0)
                    conv1 = add(add(mul(h0, v1), mul(h1, v0)), later(conv0, odd))
                    corr1 = conj_mul(h0, g1)
                    corr0 = add(add(conj_mul(h0, g0), conj_mul(h1, g1)), later(corr1, not odd))
                    spectra = (conv0, corr0, conv1, corr1)
                else:
                    cross1 = conj_mul(v0, g1)
                    cross0 = add(add(conj_mul(v0, g0), conj_mul(v1, g1)), later(cross1, not odd))
                    spectra = (cross0, cross1)
                for i, parts_of in enumerate(spectra):
                    at = slice(i * chans + r, i * chans + r + 16)
                    for col, part in zip((c, c + half // 2), parts_of):
                        prod_ref[odd, at, col : col + 128] = part.astype(BF16)
        res = res + jnp.dot(prod_ref[odd], inv_ref[bins, :], preferred_element_type=F32)
    if not home:
        for i in range(2):
            cross = res[i * chans : (i + 1) * chans] * (1.0 / half)
            cross_ref[:, i * half : (i + 1) * half] = cross.astype(BF16)
        return
    gains = jnp.concatenate([gain_ref[...]] * (half // 128), axis=1)
    scale = (2 * half) ** -0.5 / half
    for i in range(2):
        both = (res[i * rows : (i + 1) * rows] * scale + gains * x[i].astype(F32)).astype(BF16)
        for s in range(parts // 2):
            block_ref[i * (parts // 2) + s] = both[:, s * pos : (s + 1) * pos]
    for f, d, at in places(parts):
        if d:
            sent_refs[d - 1][f] = block_ref[at]
        else:
            (sib_ref if f else own_ref)[...] = block_ref[at]


def gather_kernel(*refs):
    *pair_refs, _, out_ref = refs
    for d in range(1, out_ref.shape[0] + 1):
        out_ref[d - 1] = pair_refs[-d][1]


def pair_kernel(left_ref, right_ref, out_ref):
    out_ref[...] = (left_ref[...].astype(F32) + right_ref[...].astype(F32)).astype(BF16)


def unpack_kernel(pairs, *refs):
    near_ref, val_hbm, gate_hbm, val_ref, gate_ref, turn_ref, sems = refs[pairs + 2 :]
    chans = turn_ref.shape[1] // (2 * pairs)
    for f, d, at in places(2 * pairs):
        at = pl.multiple_of(at * chans, chans)
        if f:
            both = refs[1][d - 1] if d else refs[pairs + 1][...]
        else:
            both = refs[pairs + 1 - d][0] if d else refs[0][...]
        turn_ref[0, pl.ds(at, chans), :] = both[:chans]
        turn_ref[1, pl.ds(at, chans), :] = both[chans:]
    val_ref[0] = turn_ref[1].astype(F32).T.astype(BF16)
    copies = start_copies([(val_ref, val_hbm)], sems)
    gate_ref[0] = (near_ref[0].astype(F32) * turn_ref[0].astype(F32).T).astype(BF16)
    copies += start_copies([(gate_ref, gate_hbm)], sems.at[pl.ds(1, 1)])
    for copy in copies:
        copy.wait()


def total_kernel(scale, left_ref, right_ref, _, out_hbm, out_ref, sems):
    cuts = sems.shape[0]
    each = out_ref.shape[0] // cuts
    copies = []
    for i in range(cuts):
        at = pl.ds(i * each, each)
        out_ref[at, :] = (left_ref[at, :].astype(F32) + right_ref[at, :].astype(F32)) * scale
        copies += start_copies([(out_ref.at[at, :], out_hbm.at[at, :])], sems.at[pl.ds(i, 1)])
    for copy in copies:
        copy.wait()


def call(kernel, name, outs, ins, in_specs, scratch=(), sems=0, flops=0, moved=0):
    return pl.pallas_call(
        kernel,
        out_shape=tuple(
            pltpu.VMEM(shape, dtype) if near else jax.ShapeDtypeStruct(shape, dtype)
            for shape, dtype, near in outs
        ),
        in_specs=in_specs,
        out_specs=tuple(vmem_specs(1)[0] if near else hbm_specs(1)[0] for _, _, near in outs),
        scratch_shapes=[pltpu.VMEM(s, t) for s, t in scratch]
        + ([pltpu.SemaphoreType.DMA((sems,))] if sems else []),
        compiler_params=pltpu.CompilerParams(vmem_limit_bytes=VMEM_BYTES),
        cost_estimate=pl.CostEstimate(flops=flops, bytes_accessed=moved, transcendentals=0),
        name=name,
    )(*ins)


def exchange(own, sib, name):
    pairs, rows, pos = own.shape
    got = lax.ppermute(sib, "ctx", [(j, j ^ 1) for j in range(2 * pairs)])
    sent = call(
        merge_kernel,
        "merge_" + name,
        [((2, rows, pos), BF16, True)] * (pairs - 1),
        (in_vmem(own), in_vmem(got)),
        vmem_specs(2),
        moved=8 * (pairs - 1) * rows * pos,
    )
    held = [
        lax.ppermute(sent[d - 1], "ctx", [(j, j ^ (2 * d)) for j in range(2 * pairs)])
        for d in reversed(range(1, pairs))
    ]
    return [own, got] + held


def dp_pairs(seqs, parts, step):
    masks = (step, 2 * (seqs // 2 // step) - 1)
    return [
        (s * parts + c, (s ^ masks[c % 2]) * parts + c) for s in range(seqs) for c in range(parts)
    ]


def per_device_short(values, gates, grad_out, filters, skip):
    chans, length = filters.shape
    parts = lax.axis_size("ctx")
    seqs = lax.axis_size("dp")
    _, pos, width = values.shape
    rows = 2 * chans
    fwd, inv = (jnp.asarray(table) for table in dense_tables(length // 2))
    token = ((1, pos, width), BF16)
    pairs = parts // 2
    pair_blocks = ((pairs, rows, pos), BF16)
    turned = ((2, width, pos), BF16)
    own, sib, grad_near = call(
        pack_kernel,
        "pack",
        [(*pair_blocks, True), (*pair_blocks, True), (*token, True)],
        tuple(in_hbm(x) for x in (values, gates, grad_out)),
        hbm_specs(3),
        scratch=[token, token, turned],
        sems=3,
        moved=8 * pos * width,
    )
    held = exchange(own, sib, "out")
    spec, fwd_near, inv_near, gains = call(
        filter_kernel,
        "filter_spectrum",
        [
            ((rows, length), F32, True),
            (fwd.shape, BF16, True),
            (inv.shape, BF16, True),
            ((rows, 128), F32, True),
        ],
        tuple(in_hbm(x) for x in (filters, fwd, inv)) + (skip.reshape(1, chans),),
        hbm_specs(3) + vmem_specs(1),
        scratch=[((chans, length), F32)],
        sems=3,
        flops=4 * chans * length * length,
        moved=8 * length * length,
    )
    def scratch(count):
        return [
            ((2, 2 * rows, length // 2), F32),
            ((2, count * chans, length // 2), BF16),
            ((parts, rows, pos), BF16),
        ]

    (cross,) = call(
        functools.partial(main_kernel, pairs, False),
        "filter_products",
        [((chans, length), BF16, True)],
        tuple(in_vmem(x) for x in held + [fwd_near, inv_near]),
        vmem_specs(pairs + 3),
        scratch=scratch(2),
        flops=6 * chans * length * length,
        moved=8 * length * length,
    )
    block = ((rows, pos), BF16, True)
    own, sib, *sent = call(
        functools.partial(main_kernel, pairs, True),
        "home_products",
        [block, block] + [((2, rows, pos), BF16, True)] * (pairs - 1),
        tuple(in_vmem(x) for x in held + [fwd_near, inv_near, spec, gains, cross]),
        vmem_specs(pairs + 6),
        scratch=scratch(4),
        flops=8 * chans * length * length,
        moved=8 * length * length,
    )
    came = [
        lax.ppermute(sent[d - 1], "ctx", [(j, j ^ (2 * d)) for j in range(parts)])
        for d in reversed(range(1, pairs))
    ]
    step = seqs // 2
    while step:
        other = lax.ppermute(cross, ("dp", "ctx"), dp_pairs(seqs, parts, step))
        step //= 2
        if step:
            (cross,) = call(
                pair_kernel,
                "pair_sum",
                [((chans, length), BF16, True)],
                (in_vmem(cross), in_vmem(other)),
                vmem_specs(2),
                moved=6 * chans * length,
            )
    (theirs,) = call(
        gather_kernel,
        "gather",
        [((pairs - 1, rows, pos), BF16, True)],
        tuple(in_vmem(x) for x in came + [cross]),
        vmem_specs(pairs),
        moved=4 * pairs * rows * pos,
    )
    swap = [(j, j ^ 1) for j in range(parts)]
    home = [own, lax.ppermute(theirs, "ctx", swap)] + came + [lax.ppermute(sib, "ctx", swap)]
    grad_values, grad_gates = call(
        functools.partial(unpack_kernel, pairs),
        "unpack",
        [(*token, False), (*token, False)],
        tuple(in_vmem(x) for x in home + [grad_near]),
        vmem_specs(pairs + 3),
        scratch=[token, token, turned],
        sems=2,
        moved=10 * pos * width,
    )
    (grad_filters,) = call(
        functools.partial(total_kernel, (seqs * length) ** (-0.5)),
        "total",
        [((chans, length), F32, False)],
        (in_vmem(cross), in_vmem(other), in_hbm(grad_gates)),
        vmem_specs(2) + hbm_specs(1),
        scratch=[((chans, length), F32)],
        sems=4,
        moved=8 * chans * length,
    )
    return (grad_values, grad_gates, grad_filters)


def per_device(values, gates, grad_out, filters, skip):
    chans, length = filters.shape
    pos = values.shape[1]
    seqs = lax.axis_size("dp")
    dense = length <= DENSE_LIMIT and length % 512 == 0 and chans % 16 == 0 and pos % 128 == 0
    powers = all(n > 1 and n & (n - 1) == 0 for n in (seqs, lax.axis_size("ctx")))
    if dense and powers:
        return per_device_short(values, gates, grad_out, filters, skip)
    return per_device_long(values, gates, grad_out, filters, skip)


def solution(mesh):
    in_specs = (
        P("dp", "ctx", None),
        P("dp", "ctx", None),
        P("dp", "ctx", None),
        P("ctx", None),
        P("ctx"),
    )
    out_specs = (P("dp", "ctx", None), P("dp", "ctx", None), P("ctx", None))
    return jax.shard_map(
        per_device, mesh=mesh, in_specs=in_specs, out_specs=out_specs, check_vma=False
    )
```

```python
import functools
import math

import jax
import jax.numpy as jnp
import numpy as np
from jax import lax
from jax.experimental import pallas as pl
from jax.experimental.pallas import tpu as pltpu
from jax.sharding import PartitionSpec as P

HIGH = lax.Precision.HIGHEST
BF16 = jnp.bfloat16
F32 = jnp.float32
DENSE_LIMIT = 1024
VMEM_BYTES = 16 * 2**20
UNPACK_COST = 5 * 10**9


def twiddle(rows, cols, period):
    left = lax.broadcasted_iota(jnp.int32, (rows, cols), 0)
    right = lax.broadcasted_iota(jnp.int32, (rows, cols), 1)
    angle = (left * right % period).astype(jnp.float32) * (2.0 * math.pi / period)
    return (jnp.cos(angle), jnp.sin(angle))


def pick_first(period):
    best = 2
    for cand in range(2, math.isqrt(period) + 1):
        if period % cand == 0 and cand % 2 == 0:
            best = cand
    return best


def make_tables(length):
    period = 2 * length
    first = pick_first(period)
    second = period // first
    half = first // 2
    return (
        twiddle(half, first, first),
        twiddle(first, second, period),
        twiddle(second, second, second),
        half,
        first,
        second,
        period,
    )


def forward(signal, tables):
    (cos_one, sin_one), (cos_mid, sin_mid), (cos_two, sin_two), half, first, second, period = tables
    shaped = signal.reshape(signal.shape[0], half, second)
    part_re = jnp.einsum("cmn,mk->ckn", shaped, cos_one, precision=HIGH)
    part_im = -jnp.einsum("cmn,mk->ckn", shaped, sin_one, precision=HIGH)
    mid_re = part_re * cos_mid + part_im * sin_mid
    mid_im = part_im * cos_mid - part_re * sin_mid
    spec_re = jnp.einsum("ckn,nm->ckm", mid_re, cos_two, precision=HIGH) + jnp.einsum(
        "ckn,nm->ckm", mid_im, sin_two, precision=HIGH
    )
    spec_im = jnp.einsum("ckn,nm->ckm", mid_im, cos_two, precision=HIGH) - jnp.einsum(
        "ckn,nm->ckm", mid_re, sin_two, precision=HIGH
    )
    return (spec_re, spec_im)


def inverse(spec_re, spec_im, tables):
    (cos_one, sin_one), (cos_mid, sin_mid), (cos_two, sin_two), half, first, second, period = tables
    back_re = jnp.einsum("ckm,nm->ckn", spec_re, cos_two, precision=HIGH) - jnp.einsum(
        "ckm,nm->ckn", spec_im, sin_two, precision=HIGH
    )
    back_im = jnp.einsum("ckm,nm->ckn", spec_im, cos_two, precision=HIGH) + jnp.einsum(
        "ckm,nm->ckn", spec_re, sin_two, precision=HIGH
    )
    turned_re = back_re * cos_mid - back_im * sin_mid
    turned_im = back_im * cos_mid + back_re * sin_mid
    result = jnp.einsum("ckn,mk->cmn", turned_re, cos_one, precision=HIGH) - jnp.einsum(
        "ckn,mk->cmn", turned_im, sin_one, precision=HIGH
    )
    return result.reshape(spec_re.shape[0], half * second) * (1.0 / period)


def spectral(vals_f, dz_f, filt, gains, tables, scale_a):
    vals_re, vals_im = forward(vals_f, tables)
    dz_re, dz_im = forward(dz_f, tables)
    filt_re, filt_im = forward(filt, tables)
    conv_raw = inverse(
        filt_re * vals_re - filt_im * vals_im, filt_re * vals_im + filt_im * vals_re, tables
    )
    conv = (scale_a * conv_raw + gains * vals_f).astype(BF16)
    corr = inverse(filt_re * dz_re + filt_im * dz_im, filt_re * dz_im - filt_im * dz_re, tables)
    grad_val = (scale_a * corr + gains * dz_f).astype(BF16)
    cross = inverse(vals_re * dz_re + vals_im * dz_im, vals_re * dz_im - vals_im * dz_re, tables)
    return (grad_val, conv, cross)


def per_device_long(values, gates, grad_out, filters, skip):
    length = filters.shape[1]
    scale_a = length ** (-0.5)
    scale_b = (lax.axis_size("dp") * length) ** (-0.5)
    tok_grad = grad_out[0].astype(F32)
    dz_tok = (tok_grad * gates[0].astype(F32)).astype(BF16)
    vals_ch, dz_ch = (
        lax.all_to_all(values[0].T, "ctx", split_axis=0, concat_axis=1, tiled=True),
        lax.all_to_all(dz_tok.T, "ctx", split_axis=0, concat_axis=1, tiled=True),
    )
    grad_val, conv, cross = spectral(
        vals_ch.astype(F32),
        dz_ch.astype(F32),
        filters,
        skip[:, None],
        make_tables(length),
        scale_a,
    )
    total = lax.psum(cross, "dp")
    val_back, conv_back = (
        lax.all_to_all(grad_val, "ctx", split_axis=1, concat_axis=0, tiled=True),
        lax.all_to_all(conv, "ctx", split_axis=1, concat_axis=0, tiled=True),
    )
    grad_gate_tok = (tok_grad * conv_back.T.astype(F32)).astype(BF16)
    return (val_back.T[None], grad_gate_tok[None], scale_b * total)


def dense_tables(half):
    n = np.arange(half, dtype=np.int64)[:, None]
    columns = []
    for first in range(2):
        k = np.arange(first, half, 2)[None, :]
        angle = ((2 * k + 1) * n % (4 * half)).astype(np.float64) * (math.pi / (2 * half))
        columns += [np.cos(angle), -np.sin(angle)]
    full = np.concatenate(columns, axis=1).astype(BF16)
    return full, np.ascontiguousarray(full.T)


def vmem_specs(count):
    return [pl.BlockSpec(memory_space=pltpu.VMEM)] * count


def hbm_specs(count):
    return [pl.BlockSpec(memory_space=pl.ANY)] * count


def in_vmem(array):
    return pltpu.with_memory_space_constraint(array, pltpu.VMEM)


def in_hbm(array):
    return pltpu.with_memory_space_constraint(array, pltpu.HBM)


def start_copies(pairs, sems):
    copies = [pltpu.make_async_copy(a, b, sems.at[i]) for i, (a, b) in enumerate(pairs)]
    for copy in copies:
        copy.start()
    return copies


def places(parts):
    me = lax.axis_index("ctx")
    return [
        (f, d, 2 * ((me // 2) ^ d) + ((me % 2) ^ f)) for f in range(2) for d in range(parts // 2)
    ]


def pack_kernel(
    vals_hbm, gate_hbm, grad_hbm, own_ref, sib_ref, grad_ref, vals_ref, gate_ref, turn_ref, sems
):
    pairs, rows, _ = own_ref.shape
    chans = rows // 2
    moves = [(vals_hbm, vals_ref), (gate_hbm, gate_ref), (grad_hbm, grad_ref)]
    width = vals_ref.shape[2] // 2
    halves = [pl.ds(i * width, width) for i in range(2)]
    copies = start_copies([(a.at[:, :, h], b.at[:, :, h]) for h in halves for a, b in moves], sems)
    for i, h in enumerate(halves):
        copies[3 * i].wait()
        turn_ref[0, h, :] = vals_ref[0, :, h].astype(F32).T.astype(BF16)
        copies[3 * i + 1].wait()
        copies[3 * i + 2].wait()
        dz = grad_ref[0, :, h].astype(F32) * gate_ref[0, :, h].astype(F32)
        turn_ref[1, h, :] = dz.T.astype(BF16)
    for f, d, at in places(2 * pairs):
        out_ref = sib_ref if f else own_ref
        at = pl.multiple_of(at * chans, chans)
        out_ref[d, :chans, :] = turn_ref[0, pl.ds(at, chans), :]
        out_ref[d, chans:, :] = turn_ref[1, pl.ds(at, chans), :]


def merge_kernel(own_ref, got_ref, *out_refs):
    for d, out_ref in enumerate(out_refs, 1):
        out_ref[0] = own_ref[d]
        out_ref[1] = got_ref[d]


def filter_kernel(
    filt_hbm, fwd_hbm, inv_hbm, skip_ref, spec_ref, fwd_ref, inv_ref, gain_ref, filt_ref, sems
):
    copies = start_copies([(filt_hbm, filt_ref), (fwd_hbm, fwd_ref), (inv_hbm, inv_ref)], sems)
    half = fwd_ref.shape[0]
    copies[0].wait()
    filt = jnp.concatenate([filt_ref[:, :half], filt_ref[:, half:]], axis=0)
    high = filt.astype(BF16)
    low = (filt - high.astype(F32)).astype(BF16)
    copies[1].wait()
    both = jnp.dot(
        jnp.concatenate([high, low], axis=0), fwd_ref[...], preferred_element_type=F32
    )
    spec_ref[...] = both[: filt.shape[0]] + both[filt.shape[0] :]
    chans = filt_ref.shape[0]
    row = lax.broadcasted_iota(jnp.int32, (chans, chans), 0)
    col = lax.broadcasted_iota(jnp.int32, (chans, chans), 1)
    gain = jnp.sum(jnp.where(row == col, skip_ref[...], 0.0), axis=1, keepdims=True)
    gain_ref[...] = jnp.broadcast_to(jnp.concatenate([gain, gain], axis=0), gain_ref.shape)
    copies[2].wait()


def mul(a, b):
    return (a[0] * b[0] - a[1] * b[1], a[0] * b[1] + a[1] * b[0])


def conj_mul(a, b):
    return (a[0] * b[0] + a[1] * b[1], a[0] * b[1] - a[1] * b[0])


def add(a, b):
    return (a[0] + b[0], a[1] + b[1])


def later(a, odd):
    return (a[1], -a[0]) if odd else (-a[1], a[0])


def main_kernel(pairs, *refs):
    fwd_ref, inv_ref, filt_ref, gain_ref = refs[pairs + 1 : pairs + 5]
    own_ref, sib_ref, cross_ref, spec_ref, prod_ref, block_ref = refs[pairs + 5 :]
    parts, rows, pos = block_ref.shape
    chans = rows // 2
    half = parts // 2 * pos
    for f, d, at in places(parts):
        block_ref[at] = refs[pairs + 1 - d][f] if d else refs[f][0]
    x = [
        jnp.concatenate([block_ref[s] for s in range(i, i + parts // 2)], axis=1)
        for i in (0, parts // 2)
    ]
    signals = jnp.concatenate(x, axis=0)
    res = 0.0
    for odd in range(2):
        bins = slice(odd * half, (odd + 1) * half)
        spec_ref[odd] = jnp.dot(signals, fwd_ref[:, bins], preferred_element_type=F32)
        for r in range(0, chans, 16):
            for c in range(0, half // 2, 128):

                def load(ref, row, col):
                    at = slice(row * chans + r, row * chans + r + 16)
                    return [ref[at, i + c : i + c + 128] for i in (col, col + half // 2)]

                v0, g0, v1, g1 = [load(spec_ref.at[odd], i, 0) for i in range(4)]
                h0, h1 = [load(filt_ref, i, odd * half) for i in range(2)]
                conv0 = mul(h0, v0)
                conv1 = add(add(mul(h0, v1), mul(h1, v0)), later(conv0, odd))
                corr1 = conj_mul(h0, g1)
                corr0 = add(add(conj_mul(h0, g0), conj_mul(h1, g1)), later(corr1, not odd))
                cross1 = conj_mul(v0, g1)
                cross0 = add(add(conj_mul(v0, g0), conj_mul(v1, g1)), later(cross1, not odd))
                for i, parts_of in enumerate((conv0, corr0, cross0, conv1, corr1, cross1)):
                    at = slice(i * chans + r, i * chans + r + 16)
                    for col, part in zip((c, c + half // 2), parts_of):
                        prod_ref[odd, at, col : col + 128] = part.astype(BF16)
        res = res + jnp.dot(prod_ref[odd], inv_ref[bins, :], preferred_element_type=F32)
    gains = jnp.concatenate([gain_ref[...]] * (half // 128), axis=1)
    scale = (2 * half) ** -0.5 / half
    for i in range(2):
        top = i * 3 * chans
        both = (res[top : top + rows] * scale + gains * x[i].astype(F32)).astype(BF16)
        for s in range(parts // 2):
            block_ref[i * (parts // 2) + s] = both[:, s * pos : (s + 1) * pos]
        cross = res[top + rows : top + rows + chans] * (1.0 / half)
        cross_ref[:, i * half : (i + 1) * half] = cross.astype(BF16)
    for f, d, at in places(parts):
        (sib_ref if f else own_ref)[d] = block_ref[at]


def pair_kernel(left_ref, right_ref, out_ref):
    out_ref[...] = (left_ref[...].astype(F32) + right_ref[...].astype(F32)).astype(BF16)


def unpack_kernel(pairs, *refs):
    near_ref, val_hbm, gate_hbm, val_ref, gate_ref, turn_ref, sems = refs[pairs + 1 :]
    chans = turn_ref.shape[1] // (2 * pairs)
    for f, d, at in places(2 * pairs):
        at = pl.multiple_of(at * chans, chans)
        both = refs[pairs + 1 - d][f] if d else refs[f][0]
        turn_ref[0, pl.ds(at, chans), :] = both[:chans]
        turn_ref[1, pl.ds(at, chans), :] = both[chans:]
    val_ref[0] = turn_ref[1].astype(F32).T.astype(BF16)
    copies = start_copies([(val_ref, val_hbm)], sems)
    gate_ref[0] = (near_ref[0].astype(F32) * turn_ref[0].astype(F32).T).astype(BF16)
    copies += start_copies([(gate_ref, gate_hbm)], sems.at[pl.ds(1, 1)])
    for copy in copies:
        copy.wait()


def total_kernel(scale, left_ref, right_ref, _, out_hbm, out_ref, sems):
    cuts = sems.shape[0]
    each = out_ref.shape[0] // cuts
    copies = []
    for i in range(cuts):
        at = pl.ds(i * each, each)
        out_ref[at, :] = (left_ref[at, :].astype(F32) + right_ref[at, :].astype(F32)) * scale
        copies += start_copies([(out_ref.at[at, :], out_hbm.at[at, :])], sems.at[pl.ds(i, 1)])
    for copy in copies:
        copy.wait()


def call(kernel, name, outs, ins, in_specs, scratch=(), sems=0, flops=0, moved=0):
    return pl.pallas_call(
        kernel,
        out_shape=tuple(
            pltpu.VMEM(shape, dtype) if near else jax.ShapeDtypeStruct(shape, dtype)
            for shape, dtype, near in outs
        ),
        in_specs=in_specs,
        out_specs=tuple(vmem_specs(1)[0] if near else hbm_specs(1)[0] for _, _, near in outs),
        scratch_shapes=[pltpu.VMEM(s, t) for s, t in scratch]
        + ([pltpu.SemaphoreType.DMA((sems,))] if sems else []),
        compiler_params=pltpu.CompilerParams(vmem_limit_bytes=VMEM_BYTES),
        cost_estimate=pl.CostEstimate(flops=flops, bytes_accessed=moved, transcendentals=0),
        name=name,
    )(*ins)


def exchange(own, sib, name):
    pairs, rows, pos = own.shape
    got = lax.ppermute(sib, "ctx", [(j, j ^ 1) for j in range(2 * pairs)])
    sent = call(
        merge_kernel,
        "merge_" + name,
        [((2, rows, pos), BF16, True)] * (pairs - 1),
        (in_vmem(own), in_vmem(got)),
        vmem_specs(2),
        moved=8 * (pairs - 1) * rows * pos,
    )
    held = [
        lax.ppermute(sent[d - 1], "ctx", [(j, j ^ (2 * d)) for j in range(2 * pairs)])
        for d in reversed(range(1, pairs))
    ]
    return [own, got] + held


def dp_pairs(seqs, parts, step):
    masks = (step, 2 * (seqs // 2 // step) - 1)
    return [
        (s * parts + c, (s ^ masks[c % 2]) * parts + c) for s in range(seqs) for c in range(parts)
    ]


def per_device_short(values, gates, grad_out, filters, skip):
    chans, length = filters.shape
    parts = lax.axis_size("ctx")
    seqs = lax.axis_size("dp")
    _, pos, width = values.shape
    rows = 2 * chans
    fwd, inv = (jnp.asarray(table) for table in dense_tables(length // 2))
    token = ((1, pos, width), BF16)
    pairs = parts // 2
    pair_blocks = ((pairs, rows, pos), BF16)
    turned = ((2, width, pos), BF16)
    own, sib, grad_near = call(
        pack_kernel,
        "pack",
        [(*pair_blocks, True), (*pair_blocks, True), (*token, True)],
        tuple(in_hbm(x) for x in (values, gates, grad_out)),
        hbm_specs(3),
        scratch=[token, token, turned],
        sems=6,
        moved=8 * pos * width,
    )
    held = exchange(own, sib, "out")
    spec, fwd_near, inv_near, gains = call(
        filter_kernel,
        "filter_spectrum",
        [
            ((rows, length), F32, True),
            (fwd.shape, BF16, True),
            (inv.shape, BF16, True),
            ((rows, 128), F32, True),
        ],
        tuple(in_hbm(x) for x in (filters, fwd, inv)) + (skip.reshape(1, chans),),
        hbm_specs(3) + vmem_specs(1),
        scratch=[((chans, length), F32)],
        sems=3,
        flops=4 * chans * length * length,
        moved=8 * length * length,
    )
    own, sib, cross = call(
        functools.partial(main_kernel, pairs),
        "products",
        [(*pair_blocks, True), (*pair_blocks, True), ((chans, length), BF16, True)],
        tuple(in_vmem(x) for x in held + [fwd_near, inv_near, spec, gains]),
        vmem_specs(pairs + 5),
        scratch=[
            ((2, 2 * rows, length // 2), F32),
            ((2, 3 * rows, length // 2), BF16),
            ((parts, rows, pos), BF16),
        ],
        flops=10 * chans * length * length,
        moved=8 * length * length,
    )
    home = exchange(own, sib, "home")
    step = seqs // 2
    while step:
        other = lax.ppermute(cross, ("dp", "ctx"), dp_pairs(seqs, parts, step))
        step //= 2
        if step:
            (cross,) = call(
                pair_kernel,
                "pair_sum",
                [((chans, length), BF16, True)],
                (in_vmem(cross), in_vmem(other)),
                vmem_specs(2),
                moved=6 * chans * length,
            )
    grad_values, grad_gates = call(
        functools.partial(unpack_kernel, pairs),
        "unpack",
        [(*token, False), (*token, False)],
        tuple(in_vmem(x) for x in home + [grad_near]),
        vmem_specs(pairs + 2),
        scratch=[token, token, turned],
        sems=2,
        flops=UNPACK_COST,
        moved=10 * pos * width,
    )
    (grad_filters,) = call(
        functools.partial(total_kernel, (seqs * length) ** (-0.5)),
        "total",
        [((chans, length), F32, False)],
        (in_vmem(cross), in_vmem(other), in_hbm(grad_gates)),
        vmem_specs(2) + hbm_specs(1),
        scratch=[((chans, length), F32)],
        sems=4,
        moved=8 * chans * length,
    )
    return (grad_values, grad_gates, grad_filters)


def per_device(values, gates, grad_out, filters, skip):
    chans, length = filters.shape
    pos = values.shape[1]
    seqs = lax.axis_size("dp")
    dense = length <= DENSE_LIMIT and length % 512 == 0 and chans % 16 == 0 and pos % 128 == 0
    powers = all(n > 1 and n & (n - 1) == 0 for n in (seqs, lax.axis_size("ctx")))
    if dense and powers:
        return per_device_short(values, gates, grad_out, filters, skip)
    return per_device_long(values, gates, grad_out, filters, skip)


def solution(mesh):
    in_specs = (
        P("dp", "ctx", None),
        P("dp", "ctx", None),
        P("dp", "ctx", None),
        P("ctx", None),
        P("ctx"),
    )
    out_specs = (P("dp", "ctx", None), P("dp", "ctx", None), P("ctx", None))
    return jax.shard_map(
        per_device, mesh=mesh, in_specs=in_specs, out_specs=out_specs, check_vma=False
    )
```
